512 devices in a mesh: seq: 32 (over x, z_lo, core), head: 16 (over y, z_hi).
Axes of the slice: x: 4, y: 4, z: 16 (z_hi: 4, z_lo: 4; z = z_hi * 4 + z_lo), core: 2. Of those that a mesh axis runs over, the one named last changes fastest.
Arguments:
- head_inputs: bfloat16 [2, 4096, 8192], P(None, 'seq', 'head'), may hold values from -6 to 6
- gate_inputs: bfloat16 [2, 4096, 8192], P(None, 'seq', 'head'), may hold values from -400 to 400
- write_vectors: bfloat16 [2, 4096, 8, 128], P(None, 'seq'), may hold values from -0.5 to 0.5
- read_vectors: bfloat16 [2, 4096, 8, 128], P(None, 'seq'), may hold values from -6 to 6
- step_sizes: float32 [2, 128, 4096], P(None, 'head', 'seq'), may hold values from 0.03 to 1, as said below
- decay_logs: float32 [128], P('head'), may hold values from -12 to 0
- skip_scale: float32 [128], P('head'), may hold values from 0.5 to 2
- norm_gain: float32 [8192], P('head'), may hold values from 0.1 to 1.9
- out_weight: bfloat16 [8192, 8192], P('head', 'seq'), may hold values from -0.0625 to 0.0625
- boundary: int32 [2], replicated, may hold values from 1024 to 3071
Outputs:
- mixed: bfloat16 [2, 4096, 8192], P(None, 'seq', 'head')
The draws below stay inside these ranges and needn't reach their ends.
Inputs may be any that keep to these rules, and one draw needn't show every extreme that they name: `boundary`: the first position of trajectory B; positions before it belong to trajectory A. `step_sizes`: positive.
All inputs are finite; a program needn't handle non-finite values.
Results may differ from the reference program's by a relative error of at most 0.024.
Values may be sent and summed in bfloat16 or wider, within the bound.
No kernel may reach another device: no remote copies, remote signals or barrier semaphores. Data moves between devices by JAX's collectives and lax.ppermute only.
A program may use at most 128 MiB of HBM per device.

```python
import math
import jax
import jax.numpy as jnp
from jax import lax

D = 8192
HEADS = 128
HEAD_DIM = 64
STATE = 128
GROUPS = 8
PAIRS = 2
SPAN = 128
INNER = 8192
SEQ_LEN = 4096
N_SEQ = 32
N_HEAD = 16


def draw_step_sizes(key, part):
    key = jax.random.fold_in(key, 11)
    key_rough, key_block = jax.random.split(key)
    shape = (PAIRS, HEADS, SEQ_LEN)
    rough = jax.random.uniform(key_rough, shape, jnp.float32, 0.5, 1.5)
    blocks = jnp.exp(jax.random.uniform(key_block, (PAIRS, HEADS, SEQ_LEN // SPAN, 1), jnp.float32, -math.log(2.0), math.log(2.0)))
    blocks = jnp.broadcast_to(blocks, (PAIRS, HEADS, SEQ_LEN // SPAN, SPAN)).reshape(shape)
    return (0.25 * rough * blocks).astype(jnp.float32)


def draw_decay_logs(key, part):
    key = jax.random.fold_in(key, 12)
    key_pick, key_fast, key_slow = jax.random.split(key, 3)
    share = 0.5
    quick = jax.random.uniform(key_pick, (HEADS,), jnp.float32) < share
    fast_rate = jax.random.uniform(key_fast, (HEADS,), jnp.float32, 1.0 / 50.0, 1.0 / 30.0)
    slow_rate = jnp.exp(jax.random.uniform(key_slow, (HEADS,), jnp.float32, math.log(0.2), 0.0)) / SEQ_LEN
    rates = jnp.where(quick, fast_rate, slow_rate)
    return jnp.log(rates / 0.25).astype(jnp.float32)


def draw_gate_inputs(key, part):
    key = jax.random.fold_in(key, 13)
    key_base, key_rows = jax.random.split(key)
    shape = (PAIRS, SEQ_LEN, INNER)
    column = (jnp.arange(INNER) // HEAD_DIM).astype(jnp.float32) / HEADS
    base = jnp.clip(jax.random.normal(key_base, shape, jnp.float32), -4.0, 4.0)
    columns = jnp.exp(column * math.log(10.0))
    rows_scale = jnp.exp(jax.random.uniform(key_rows, (PAIRS, SEQ_LEN, 1), jnp.float32, 0.0, math.log(10.0)))
    return (0.5 * base * columns * rows_scale).astype(jnp.bfloat16)


def levels(rng, dims, shards, least, high):
    factor_of = 1.0
    for dim, blocks in shards:
        draws = jax.random.uniform(jax.random.fold_in(jax.random.fold_in(rng, 6), dim), (blocks,), jnp.float32, least / len(shards), high / len(shards))
        factor_of = factor_of * jnp.repeat(jnp.exp(draws), dims[dim] // blocks).reshape((-1,) + (1,) * (len(dims) - 1 - dim))
    return factor_of


def noise(rng, extent, deviation, bound, shards=(), kind=jnp.bfloat16):
    loudness = levels(rng, extent, shards, -0.22, 0.18) if shards else 1.0
    entries = jax.random.normal(rng, extent, jnp.float32) * deviation * loudness
    return jnp.minimum(jnp.maximum(entries, -bound), bound).astype(kind)


def setup_inputs(seed: int = 0) -> dict:
    streams_of = jax.random.split(jax.random.key(seed), 11)
    return {
        "head_inputs": noise(streams_of[0], (PAIRS, SEQ_LEN, INNER), 1.0, 6.0, ((1, 32), (2, 16))),
        "gate_inputs": draw_gate_inputs(jax.random.fold_in(streams_of[10], 71), 0),
        "write_vectors": noise(streams_of[2], (PAIRS, SEQ_LEN, GROUPS, STATE), STATE ** -0.5, 0.5, ((1, 32),)),
        "read_vectors": noise(streams_of[3], (PAIRS, SEQ_LEN, GROUPS, STATE), 1.0, 6.0, ((1, 32),)),
        "step_sizes": draw_step_sizes(jax.random.fold_in(streams_of[10], 71), 0),
        "decay_logs": draw_decay_logs(jax.random.fold_in(streams_of[10], 71), 0),
        "skip_scale": jnp.clip(0.5 + 1.5 * jax.random.uniform(streams_of[6], (HEADS,), jnp.float32) ** levels(streams_of[6], (HEADS,), ((0, 16),), -0.2, 0.2), 0.5, 2.0),
        "norm_gain": jnp.clip(1.0 + 0.18 * jax.random.normal(streams_of[7], (INNER,), jnp.float32), 0.1, 1.9),
        "out_weight": noise(streams_of[8], (INNER, D), INNER ** -0.5, 0.0625, ((0, 16), (1, 32))),
        "boundary": jax.random.randint(streams_of[9], (PAIRS,), SEQ_LEN // 4, 3 * SEQ_LEN // 4).astype(jnp.int32),
    }


epsilon = 1e-05

def rounded(values):
    return lax.optimization_barrier(values.astype(jnp.bfloat16)).astype(jnp.float32)

def reference(head_inputs, gate_inputs, write_vectors, read_vectors, step_sizes, decay_logs, skip_scale, norm_gain, out_weight, boundary):
    pair_count = head_inputs.shape[0]
    per_group = HEADS // GROUPS
    block_count = N_SEQ
    block_len = SPAN
    position = jnp.arange(SEQ_LEN, dtype=jnp.int32)
    parts = (position[None, :] >= boundary[:, None]).astype(jnp.float32).reshape(pair_count, block_count, block_len)
    before = jnp.arange(block_count, dtype=jnp.int32) * block_len - 1
    previous = (before[None, :] >= boundary[:, None]).astype(jnp.float32)
    rates = jnp.exp(decay_logs)
    steps = step_sizes.reshape(pair_count, HEADS, block_count, block_len)
    cumul = jnp.cumsum(-rates[None, :, None, None] * steps, axis=-1)
    lower = jnp.arange(block_len)[:, None] >= jnp.arange(block_len)[None, :]
    same = (parts[:, :, :, None] == parts[:, :, None, :]) & lower
    diffs = cumul[..., :, None] - cumul[..., None, :]
    decay = jnp.where(same[:, None], jnp.exp(jnp.minimum(diffs, 0.0)), 0.0)
    decay = decay.reshape(pair_count, GROUPS, per_group, block_count, block_len, block_len).transpose(0, 3, 1, 2, 4, 5)
    step_group = steps.reshape(pair_count, GROUPS, per_group, block_count, block_len).transpose(0, 3, 1, 2, 4)
    inputs = head_inputs.reshape(pair_count, block_count, block_len, GROUPS, per_group, HEAD_DIM).astype(jnp.float32)
    writes = write_vectors.reshape(pair_count, block_count, block_len, GROUPS, STATE).astype(jnp.float32)
    reads = read_vectors.reshape(pair_count, block_count, block_len, GROUPS, STATE).astype(jnp.float32)
    scores = jnp.einsum('pkign,pkjgn->pkgij', reads, writes)
    mixing = rounded(scores[:, :, :, None] * decay * step_group[:, :, :, :, None, :])
    intra = jnp.einsum('pkglij,pkjgld->pkigld', mixing, inputs)
    ends = jnp.where(parts[:, :, -1:] == parts, 1.0, 0.0)
    end_weights = jnp.exp(cumul[..., -1:] - cumul) * ends[:, None] * steps
    end_weights = end_weights.reshape(pair_count, GROUPS, per_group, block_count, block_len).transpose(0, 3, 4, 1, 2)
    weighted = rounded(writes[:, :, :, :, None, :] * end_weights[..., None])
    block_state = jnp.einsum('pkjgln,pkjgld->kpglnd', weighted, inputs)
    passing = jnp.exp(cumul[..., -1]) * (parts[:, :, -1] == previous).astype(jnp.float32)[:, None]
    passing = passing.reshape(pair_count, GROUPS, per_group, block_count).transpose(3, 0, 1, 2)

    def advance(carried, items):
        factor_now, fresh = items
        return (factor_now[..., None, None] * carried + fresh, carried)
    start_state = jnp.zeros(block_state.shape[1:], jnp.float32)
    _, incoming = lax.scan(advance, start_state, (passing, block_state))
    carry = jnp.einsum('pkign,kpglnd->pkigld', reads, incoming, precision=lax.Precision.HIGHEST)
    factor = jnp.exp(cumul) * (parts == previous[:, :, None]).astype(jnp.float32)[:, None]
    factor = factor.reshape(pair_count, GROUPS, per_group, block_count, block_len).transpose(0, 3, 4, 1, 2)[..., None]
    skip_group = skip_scale.reshape(GROUPS, per_group)[:, :, None]
    ssm = intra + carry * factor + skip_group * inputs
    gated = ssm.reshape(pair_count, SEQ_LEN, INNER) * jax.nn.silu(gate_inputs.astype(jnp.float32))
    meansq = lax.optimization_barrier(jnp.sum(gated * gated, axis=-1)) / INNER
    hidden = (gated * lax.rsqrt(meansq + epsilon)[..., None] * norm_gain).astype(jnp.bfloat16)
    hidden = hidden.reshape(pair_count * SEQ_LEN, INNER)
    block_width = INNER // N_HEAD

    def add_block(index, summed):
        features = lax.dynamic_slice_in_dim(hidden, index * block_width, block_width, 1)
        rows_now = lax.dynamic_slice_in_dim(out_weight, index * block_width, block_width, 0)
        partial_value = jnp.dot(features, rows_now, preferred_element_type=jnp.float32)
        return summed + rounded(partial_value)
    summed = lax.fori_loop(0, N_HEAD, add_block, jnp.zeros((pair_count * SEQ_LEN, D), jnp.float32))
    return summed.astype(jnp.bfloat16).reshape(pair_count, SEQ_LEN, D)
```

```python
import jax
import jax.numpy as jnp
from jax import lax
from jax.experimental import pallas as pl
from jax.experimental.pallas import tpu as pltpu
from jax.sharding import PartitionSpec as P

INNER = 8192
EPSILON = 1e-05
PAIRS = 2
SPAN = 128
HEADS_LOCAL = 8
HALF = 4
CHANNELS = 64
STATE = 128
WIDTH = 512
TOKENS = PAIRS * SPAN
STATE_ROWS = PAIRS * HALF * CHANNELS
PAYLOAD_ROWS = STATE_ROWS + 16
TOKEN_ROWS = TOKENS + 16
NX = NZL = NCORE = NY = NZH = 4
NCORE = 2
EXACT = lax.Precision.HIGHEST
f32 = jnp.float32
bf16 = jnp.bfloat16


def seq_index(x, zl, core):
    return (x * NZL + zl) * NCORE + core


def head_index(y, zh):
    return y * NZH + zh


def route(move):
    pairs = []
    for x in range(NX):
        for zl in range(NZL):
            for core in range(NCORE):
                for y in range(NY):
                    for zh in range(NZH):
                        to = move(x, zl, core, y, zh)
                        if to is None:
                            continue
                        source = seq_index(x, zl, core) * NY * NZH + head_index(y, zh)
                        target = seq_index(*to[:3]) * NY * NZH + head_index(*to[3:])
                        pairs.append((source, target))
    return pairs


def send(value, move):
    return lax.ppermute(value, ("seq", "head"), route(move))


def to_core(value):
    return send(value, lambda x, zl, c, y, zh: (x, zl, 1 - c, y, zh))


def to_zl(value, d):
    return send(value, lambda x, zl, c, y, zh: (x, (zl + d) % NZL, c, y, zh))


def to_x(value, d):
    return send(value, lambda x, zl, c, y, zh: (x + d, zl, c, y, zh) if x + d < NX else None)


def to_y(value, d):
    return send(value, lambda x, zl, c, y, zh: (x, zl, c, (y + d) % NY, zh))


def to_zh(value, d):
    return send(value, lambda x, zl, c, y, zh: (x, zl, c, y, (zh + d) % NZH))


def swap_z(value):
    return send(value, lambda x, zl, c, y, zh: (x, zh, c, y, zl))


VMEM = pl.BlockSpec(memory_space=pltpu.VMEM)
SMEM = pl.BlockSpec(memory_space=pltpu.SMEM)


def call(kernel, outs, specs, args, flops, moved, limit=None):
    return pl.pallas_call(
        kernel,
        out_shape=outs,
        in_specs=specs,
        out_specs=jax.tree.map(lambda _: VMEM, outs),
        cost_estimate=pl.CostEstimate(flops=flops, bytes_accessed=moved, transcendentals=0),
        compiler_params=pltpu.CompilerParams(vmem_limit_bytes=limit or 16 * 2**20),
    )(*args)


def shape(dims, kind):
    return jax.ShapeDtypeStruct(dims, kind)


def head_rows(scalars):
    rows = lax.broadcasted_iota(jnp.int32, (HEADS_LOCAL, SPAN), 0)
    out = jnp.zeros((HEADS_LOCAL, SPAN), f32)
    for h in range(HEADS_LOCAL):
        out = jnp.where(rows == h, scalars[h], out)
    return out


def split(value):
    high = value.astype(bf16)
    low = (value - high.astype(f32)).astype(bf16)
    return high, low


def flag(condition):
    return jnp.where(condition, 1.0, 0.0).astype(f32)


def states_kernel(meta, decay_logs, x, writes, steps, out, mine, decay_mine):
    first, core = meta[0], meta[1]
    rates = jnp.exp(head_rows(decay_logs))
    row = lax.broadcasted_iota(jnp.int32, (SPAN, SPAN), 0)
    col = lax.broadcasted_iota(jnp.int32, (SPAN, SPAN), 1)
    upto = jnp.where(row <= col, 1.0, 0.0).astype(f32)
    position = first + lax.broadcasted_iota(jnp.int32, (HEADS_LOCAL, SPAN), 1)
    send_decay, keep_decay = [], []
    rows = HALF * CHANNELS
    for p in range(PAIRS):
        limit = meta[2 + p]
        step = steps[p]
        cumul = jnp.dot(-rates * step, upto, precision=EXACT, preferred_element_type=f32)
        last = cumul[:, SPAN - 1 :]
        last_part = jnp.where(first + SPAN - 1 >= limit, 1, 0)
        previous = jnp.where(first - 1 >= limit, 1, 0)
        part = jnp.where(position >= limit, 1, 0)
        ends = jnp.exp(last - cumul) * step
        ends = jnp.where(part == last_part, ends, 0.0)
        spread = jnp.broadcast_to(ends[:, None, :], (HEADS_LOCAL, CHANNELS, SPAN))
        spread = spread.reshape(HEADS_LOCAL * CHANNELS, SPAN)
        turned = x[p].astype(f32).T
        state = jnp.dot(
            (turned * spread).astype(bf16), writes[p], preferred_element_type=f32
        )
        passing = jnp.broadcast_to(jnp.exp(last), (HEADS_LOCAL, SPAN))
        passing = jnp.where(last_part == previous, passing, 0.0)
        here = pl.ds(p * rows, rows)
        lower, upper = state[:rows], state[rows:]
        out[here, :] = jnp.where(core == 0, upper, lower).astype(bf16)
        mine[here, :] = jnp.where(core == 0, lower, upper)
        send_decay.append(jnp.where(core == 0, passing[HALF:], passing[:HALF]))
        keep_decay.append(jnp.where(core == 0, passing[:HALF], passing[HALF:]))
    leaving = jnp.concatenate(send_decay, axis=0)
    high = leaving.astype(bf16).astype(f32)
    out[pl.ds(STATE_ROWS, 16), :] = jnp.concatenate([high, leaving - high], axis=0).astype(bf16)
    decay_mine[...] = jnp.concatenate(keep_decay, axis=0)


def unpack(ref):
    tail = ref[pl.ds(STATE_ROWS, 16), :].astype(f32)
    return tail[:8] + tail[8:], ref[pl.ds(0, STATE_ROWS), :].astype(f32)


def scale(decay, state):
    groups = PAIRS * HALF
    return (state.reshape(groups, CHANNELS, STATE) * decay[:, None, :]).reshape(STATE_ROWS, STATE)


def pack(out, decay, state):
    out[pl.ds(0, STATE_ROWS), :] = state.astype(bf16)
    high = decay.astype(bf16).astype(f32)
    out[pl.ds(STATE_ROWS, 16), :] = jnp.concatenate([high, decay - high], axis=0).astype(bf16)


def chip_kernel(meta, got, mine, decay_mine, total, state_first, decay_first):
    core = meta[1]
    decay_got, state_got = unpack(got)
    decay_own, state_own = decay_mine[...], mine[...]
    decay0 = jnp.where(core == 0, decay_own, decay_got)
    decay1 = jnp.where(core == 0, decay_got, decay_own)
    state0 = jnp.where(core == 0, state_own, state_got)
    state1 = jnp.where(core == 0, state_got, state_own)
    state_first[...] = state0
    decay_first[...] = decay0
    pack(total, decay0 * decay1, scale(decay1, state0) + state1)


def line_kernel(meta, own, from1, from2, from3, total, state_before, decay_before):
    zl = meta[4]
    state = jnp.zeros((STATE_ROWS, STATE), f32)
    decay = jnp.ones((PAIRS * HALF, STATE), f32)

    def follow(decay, state, ref, valid):
        factor, fresh = unpack(ref)
        factor = jnp.where(valid, factor, 1.0)
        fresh = jnp.where(valid, fresh, 0.0)
        return decay * factor, scale(factor, state) + fresh

    apart = ((3, from3), (2, from2), (1, from1))
    for d, ref in apart:
        decay, state = follow(decay, state, ref, zl >= d)
    state_before[...] = state
    decay_before[...] = decay
    factor, fresh = unpack(own)
    decay, state = decay * factor, scale(factor, state) + fresh
    for d, ref in apart:
        decay, state = follow(decay, state, ref, zl < d)
    pack(total, decay, state)


def whole_kernel(
    meta, from1, from2, from3, state_before, decay_before, state_first, decay_first, out, keep
):
    core = meta[1]
    state = jnp.zeros((STATE_ROWS, STATE), f32)
    for ref in (from3, from2, from1):
        factor, fresh = unpack(ref)
        state = scale(factor, state) + fresh
    entering = scale(decay_before[...], state) + state_before[...]
    second = scale(decay_first[...], entering) + state_first[...]
    out[...] = jnp.where(core == 0, second, entering).astype(bf16)
    keep[...] = jnp.where(core == 0, entering, second).astype(bf16)


def inside_kernel(
    meta, decay_logs, skip_scale, x, writes, reads, steps, gates, early, late
):
    first = meta[0]
    rates = jnp.exp(head_rows(decay_logs))
    row = lax.broadcasted_iota(jnp.int32, (SPAN, SPAN), 0)
    col = lax.broadcasted_iota(jnp.int32, (SPAN, SPAN), 1)
    upto = jnp.where(row <= col, 1.0, 0.0).astype(f32)
    below = jnp.where(row >= col, 1.0, 0.0).astype(f32)
    for p in range(PAIRS):
        limit = meta[2 + p]
        step = steps[p]
        drop = -rates * step
        cumul = jnp.dot(drop, upto, precision=EXACT, preferred_element_type=f32)
        turned = lax.dot_general(
            below, drop, (((1,), (1,)), ((), ())), precision=EXACT, preferred_element_type=f32
        )
        part_row = jnp.where(first + row >= limit, 1, 0)
        part_col = jnp.where(first + col >= limit, 1, 0)
        previous = jnp.where(first - 1 >= limit, 1, 0)
        allowed = (part_row == part_col) & (row >= col)
        scores = lax.dot_general(
            reads[p], writes[p], (((1,), (1,)), ((), ())), preferred_element_type=f32
        )
        scores = jnp.where(allowed, scores, 0.0)
        reached = jnp.where(part_row[:, :CHANNELS] == previous, 1.0, 0.0)
        for h in range(HEADS_LOCAL):
            here = slice(h * CHANNELS, (h + 1) * CHANNELS)
            column = turned[:, h : h + 1]
            decay = jnp.exp(jnp.minimum(column - cumul[h : h + 1, :], 0.0))
            weights = (scores * decay * step[h : h + 1, :]).astype(bf16)
            inputs = x[p, :, here]
            intra = jnp.dot(weights, inputs, preferred_element_type=f32)
            ssm = intra + skip_scale[h] * inputs.astype(f32)
            gate = gates[p, :, here].astype(f32)
            opened = gate / (1.0 + jnp.exp(-gate))
            early[p, :, here] = ssm * opened
            late[p, :, here] = opened * reached * jnp.exp(column)


def hidden_kernel(meta, keep, got, reads, early, late, gain, out):
    core = meta[1]
    rows = HALF * CHANNELS
    ones = jnp.ones((8, WIDTH), f32)
    highs, lows = [], []
    for p in range(PAIRS):
        here = pl.ds(p * rows, rows)
        own, other = keep[here, :], got[here, :]
        total = jnp.zeros((8, SPAN), f32)
        for half in range(2):
            state = jnp.where(core == half, own, other)
            columns = slice(half * rows, (half + 1) * rows)
            carry = lax.dot_general(
                reads[p], state, (((1,), (1,)), ((), ())), preferred_element_type=f32
            )
            gated = early[p, :, columns] + late[p, :, columns] * carry
            out[pl.ds(p * SPAN, SPAN), columns] = (gated * gain[:, columns]).astype(bf16)
            total += lax.dot_general(
                ones[:, columns],
                gated * gated,
                (((1,), (1,)), ((), ())),
                precision=EXACT,
                preferred_element_type=f32,
            )
        high = total.astype(bf16).astype(f32)
        highs.append(high)
        lows.append(total - high)
    squares = jnp.concatenate(highs + lows, axis=1)
    out[pl.ds(TOKENS, 16), :] = jnp.concatenate([squares, squares], axis=0).astype(bf16)


def project_kernel(index, own, up, down, far, weight, out):
    half = pl.program_id(0)
    total = jnp.zeros((TOKENS, WIDTH // 2), f32)
    squares = jnp.zeros((16, TOKENS), f32)
    for k, ref in enumerate((own, up, down, far)):
        total += jnp.dot(
            ref[pl.ds(0, TOKENS), :], weight[0, index[1 + k], 0], preferred_element_type=f32
        )
        tail = ref[pl.ds(TOKENS, 16), :].astype(f32)
        squares += tail[:, :TOKENS] + tail[:, TOKENS:]
    out[pl.ds(0, TOKENS), :] = total.astype(bf16)
    high = squares.astype(bf16).astype(f32)
    out[pl.ds(TOKENS, 16), :] = jnp.where(half == 0, high, squares - high).astype(bf16)


def project(index, parts, weight):
    whole = pl.BlockSpec((TOKEN_ROWS, WIDTH), lambda half, index: (0, 0))
    return pl.pallas_call(
        project_kernel,
        out_shape=shape((TOKEN_ROWS, WIDTH), bf16),
        grid_spec=pltpu.PrefetchScalarGridSpec(
            num_scalar_prefetch=1,
            grid=(2,),
            in_specs=[whole] * 4
            + [
                pl.BlockSpec(
                    (1, NZH, 1, WIDTH, WIDTH // 2),
                    lambda half, index: (index[0], 0, half, 0, 0),
                )
            ],
            out_specs=pl.BlockSpec((TOKEN_ROWS, WIDTH // 2), lambda half, index: (0, half)),
        ),
        cost_estimate=pl.CostEstimate(
            flops=2 * TOKENS * WIDTH * 4 * WIDTH, bytes_accessed=3 * 2**20, transcendentals=0
        ),
        compiler_params=pltpu.CompilerParams(vmem_limit_bytes=16 * 2**20),
    )(index, *parts, weight)


def finish_kernel(own, got1, got2, got3, out):
    refs = (own, got1, got2, got3)
    squares = jnp.zeros((16, TOKENS), f32)
    for ref in refs:
        tail = ref[pl.ds(TOKENS, 16), :].astype(f32)
        squares += tail[:, :TOKENS] + tail[:, TOKENS:]
    factor = lax.rsqrt(squares[:8] / INNER + EPSILON)
    row = lax.broadcasted_iota(jnp.int32, (SPAN, SPAN), 0)
    col = lax.broadcasted_iota(jnp.int32, (SPAN, SPAN), 1)
    same = jnp.where(row == col, 1.0, 0.0).astype(f32)
    for p in range(PAIRS):
        here = pl.ds(p * SPAN, SPAN)
        turned = lax.dot_general(
            same,
            factor[:, p * SPAN : (p + 1) * SPAN],
            (((1,), (1,)), ((), ())),
            precision=EXACT,
            preferred_element_type=f32,
        )
        total = sum(ref[here, :].astype(f32) for ref in refs)
        out[p] = (total * turned[:, :1]).astype(bf16)


def shards(
    head_inputs,
    gate_inputs,
    write_vectors,
    read_vectors,
    step_sizes,
    decay_logs,
    skip_scale,
    norm_gain,
    out_weight,
    boundary,
):
    seq, head = lax.axis_index("seq"), lax.axis_index("head")
    zl, core = (seq // NCORE) % NZL, seq % NCORE
    y, zh = head // NZH, head % NZH
    first = seq * SPAN
    meta = jnp.concatenate(
        [jnp.stack([first, core]).astype(jnp.int32), boundary, jnp.stack([zl, zh]).astype(jnp.int32)]
    )

    weight = lax.all_gather(swap_z(out_weight), "seq", axis=0, tiled=True)
    weight = weight.reshape(NY, NZH, NCORE, WIDTH, WIDTH // 2)

    group = head // 2
    writes = lax.dynamic_index_in_dim(write_vectors, group, 2, keepdims=False)
    reads = lax.dynamic_index_in_dim(read_vectors, group, 2, keepdims=False)

    payload = shape((PAYLOAD_ROWS, STATE), bf16)
    wide = shape((STATE_ROWS, STATE), f32)
    small = shape((PAIRS * HALF, STATE), f32)
    leaving, mine, decay_mine = call(
        states_kernel,
        (payload, wide, small),
        [SMEM, SMEM, VMEM, VMEM, VMEM],
        (meta, decay_logs, head_inputs, writes, step_sizes),
        2 * 2**24,
        2**20,
    )
    total, state_first, decay_first = call(
        chip_kernel,
        (payload, wide, small),
        [SMEM, VMEM, VMEM, VMEM],
        (meta, to_core(leaving), mine, decay_mine),
        2**18,
        2**19,
    )
    line, state_before, decay_before = call(
        line_kernel,
        (payload, wide, small),
        [SMEM] + [VMEM] * 4,
        (meta, total, to_zl(total, 1), to_zl(total, 2), to_zl(total, 3)),
        2**18,
        2**19,
    )
    half_state = shape((STATE_ROWS, STATE), bf16)
    crossing, keep = call(
        whole_kernel,
        (half_state, half_state),
        [SMEM] + [VMEM] * 7,
        (meta, to_x(line, 1), to_x(line, 2), to_x(line, 3))
        + (state_before, decay_before, state_first, decay_first),
        2**18,
        2**19,
    )
    got = to_core(crossing)

    local = shape((PAIRS, SPAN, WIDTH), f32)
    early, late = call(
        inside_kernel,
        (local, local),
        [SMEM, SMEM, SMEM] + [VMEM] * 5,
        (meta, decay_logs, skip_scale, head_inputs, writes, reads, step_sizes, gate_inputs),
        2**26,
        2**21,
    )
    hidden = call(
        hidden_kernel,
        shape((TOKEN_ROWS, WIDTH), bf16),
        [SMEM] + [VMEM] * 6,
        (meta, keep, got, reads, early, late, norm_gain.reshape(1, WIDTH)),
        2**25,
        2**21,
    )
    parts = (hidden, to_zh(hidden, 1), to_zh(hidden, NZH - 1), to_zh(hidden, 2))
    blocks = [zh, (zh + NZH - 1) % NZH, (zh + 1) % NZH, (zh + 2) % NZH]

    def partial(d):
        index = jnp.stack([(y + d) % NY] + blocks).astype(jnp.int32)
        return project(index, parts, weight)

    arrived = [to_y(partial(d), d) for d in (2, 1, 3)]
    return call(
        finish_kernel,
        shape((PAIRS, SPAN, WIDTH), bf16),
        [VMEM] * 4,
        (partial(0), *arrived),
        2**20,
        2**20,
    )


def solution(mesh):
    return jax.shard_map(
        shards,
        mesh=mesh,
        in_specs=(
            P(None, "seq", "head"),
            P(None, "seq", "head"),
            P(None, "seq", None, None),
            P(None, "seq", None, None),
            P(None, "head", "seq"),
            P("head"),
            P("head"),
            P("head"),
            P("head", "seq"),
            P(),
        ),
        out_specs=P(None, "seq", "head"),
        check_vma=False,
    )
```

```python
import jax
import jax.numpy as jnp
from jax import lax
from jax.experimental import pallas as pl
from jax.experimental.pallas import tpu as pltpu
from jax.sharding import PartitionSpec as P

INNER = 8192
EPSILON = 1e-05
PAIRS = 2
SPAN = 128
HEADS_LOCAL = 8
HALF = 4
CHANNELS = 64
STATE = 128
WIDTH = 512
TOKENS = PAIRS * SPAN
STATE_ROWS = PAIRS * HALF * CHANNELS
PAYLOAD_ROWS = STATE_ROWS + 16
SPOT = ((0, 2, 3, 1), (1, 2, 3, 0), (3, 0, 1, 2), (2, 0, 1, 3))
TOKEN_ROWS = TOKENS + 16
NX = NZL = NY = NZH = 4
NCORE = 2
EXACT = lax.Precision.HIGHEST
f32 = jnp.float32
bf16 = jnp.bfloat16


def seq_index(x, zl, core):
    return (x * NZL + zl) * NCORE + core


def head_index(y, zh):
    return y * NZH + zh


def route(move):
    pairs = []
    for x in range(NX):
        for zl in range(NZL):
            for core in range(NCORE):
                for y in range(NY):
                    for zh in range(NZH):
                        to = move(x, zl, core, y, zh)
                        if to is None:
                            continue
                        source = seq_index(x, zl, core) * NY * NZH + head_index(y, zh)
                        target = seq_index(*to[:3]) * NY * NZH + head_index(*to[3:])
                        pairs.append((source, target))
    return pairs


def send(value, move):
    return lax.ppermute(value, ("seq", "head"), route(move))


def to_core(value):
    return send(value, lambda x, zl, c, y, zh: (x, zl, 1 - c, y, zh))


def to_zl(value, d):
    return send(value, lambda x, zl, c, y, zh: (x, (zl + d) % NZL, c, y, zh))


def to_x(value, d):
    return send(value, lambda x, zl, c, y, zh: (x + d, zl, c, y, zh) if x + d < NX else None)


def to_y(value, d):
    return send(value, lambda x, zl, c, y, zh: (x, zl, c, (y + d) % NY, zh))


def to_zh(value, d):
    return send(value, lambda x, zl, c, y, zh: (x, zl, c, y, (zh + d) % NZH))


def swap_z(value):
    return send(value, lambda x, zl, c, y, zh: (x, SPOT[zl][zh], c, y, zl))


def gather(block, key):
    groups = {}
    for x in range(NX):
        for zl in range(NZL):
            for core in range(NCORE):
                groups.setdefault(key(x, zl, core), []).append(seq_index(x, zl, core))
    return lax.all_gather(
        block, "seq", axis=0, tiled=True, axis_index_groups=list(groups.values())
    )


VMEM = pl.BlockSpec(memory_space=pltpu.VMEM)
SMEM = pl.BlockSpec(memory_space=pltpu.SMEM)


def call(kernel, outs, specs, args, flops, moved, scratch=(), limit=16 * 2**20):
    return pl.pallas_call(
        kernel,
        out_shape=outs,
        in_specs=specs,
        out_specs=jax.tree.map(lambda _: VMEM, outs),
        scratch_shapes=scratch,
        cost_estimate=pl.CostEstimate(flops=flops, bytes_accessed=moved, transcendentals=0),
        compiler_params=pltpu.CompilerParams(vmem_limit_bytes=limit),
    )(*args)


def shape(dims, kind):
    return jax.ShapeDtypeStruct(dims, kind)


def head_rows(scalars):
    rows = lax.broadcasted_iota(jnp.int32, (HEADS_LOCAL, SPAN), 0)
    out = jnp.zeros((HEADS_LOCAL, SPAN), f32)
    for h in range(HEADS_LOCAL):
        out = jnp.where(rows == h, scalars[h], out)
    return out


def states_kernel(meta, decay_logs, x, writes, steps, out, mine, decay_mine):
    first, core = meta[0], meta[1]
    rates = jnp.exp(head_rows(decay_logs))
    row = lax.broadcasted_iota(jnp.int32, (SPAN, SPAN), 0)
    col = lax.broadcasted_iota(jnp.int32, (SPAN, SPAN), 1)
    upto = jnp.where(row <= col, 1.0, 0.0).astype(f32)
    position = first + lax.broadcasted_iota(jnp.int32, (HEADS_LOCAL, SPAN), 1)
    send_decay, keep_decay = [], []
    rows = HALF * CHANNELS
    for p in range(PAIRS):
        limit = meta[2 + p]
        step = steps[p]
        cumul = jnp.dot(-rates * step, upto, precision=EXACT, preferred_element_type=f32)
        last = cumul[:, SPAN - 1 :]
        last_part = jnp.where(first + SPAN - 1 >= limit, 1, 0)
        previous = jnp.where(first - 1 >= limit, 1, 0)
        part = jnp.where(position >= limit, 1, 0)
        ends = jnp.exp(last - cumul) * step
        ends = jnp.where(part == last_part, ends, 0.0)
        spread = jnp.broadcast_to(ends[:, None, :], (HEADS_LOCAL, CHANNELS, SPAN))
        spread = spread.reshape(HEADS_LOCAL * CHANNELS, SPAN)
        turned = x[p].astype(f32).T
        state = jnp.dot(
            (turned * spread).astype(bf16), writes[p], preferred_element_type=f32
        )
        passing = jnp.broadcast_to(jnp.exp(last), (HEADS_LOCAL, SPAN))
        passing = jnp.where(last_part == previous, passing, 0.0)
        here = pl.ds(p * rows, rows)
        lower, upper = state[:rows], state[rows:]
        out[here, :] = jnp.where(core == 0, upper, lower).astype(bf16)
        mine[here, :] = jnp.where(core == 0, lower, upper)
        send_decay.append(jnp.where(core == 0, passing[HALF:], passing[:HALF]))
        keep_decay.append(jnp.where(core == 0, passing[:HALF], passing[HALF:]))
    leaving = jnp.concatenate(send_decay, axis=0)
    high = leaving.astype(bf16).astype(f32)
    out[pl.ds(STATE_ROWS, 16), :] = jnp.concatenate([high, leaving - high], axis=0).astype(bf16)
    decay_mine[...] = jnp.concatenate(keep_decay, axis=0)


def unpack(ref):
    tail = ref[pl.ds(STATE_ROWS, 16), :].astype(f32)
    return tail[:8] + tail[8:], ref[pl.ds(0, STATE_ROWS), :].astype(f32)


def scale(decay, state):
    groups = PAIRS * HALF
    return (state.reshape(groups, CHANNELS, STATE) * decay[:, None, :]).reshape(STATE_ROWS, STATE)


def pack(out, decay, state):
    out[pl.ds(0, STATE_ROWS), :] = state.astype(bf16)
    high = decay.astype(bf16).astype(f32)
    out[pl.ds(STATE_ROWS, 16), :] = jnp.concatenate([high, decay - high], axis=0).astype(bf16)


def chip_kernel(meta, got, mine, decay_mine, total, state_first, decay_first):
    core = meta[1]
    decay_got, state_got = unpack(got)
    decay_own, state_own = decay_mine[...], mine[...]
    decay0 = jnp.where(core == 0, decay_own, decay_got)
    decay1 = jnp.where(core == 0, decay_got, decay_own)
    state0 = jnp.where(core == 0, state_own, state_got)
    state1 = jnp.where(core == 0, state_got, state_own)
    state_first[...] = state0
    decay_first[...] = decay0
    pack(total, decay0 * decay1, scale(decay1, state0) + state1)


def line_kernel(meta, own, from1, from2, from3, total, state_before, decay_before):
    zl = meta[4]
    state = jnp.zeros((STATE_ROWS, STATE), f32)
    decay = jnp.ones((PAIRS * HALF, STATE), f32)

    def follow(decay, state, ref, valid):
        factor, fresh = unpack(ref)
        factor = jnp.where(valid, factor, 1.0)
        fresh = jnp.where(valid, fresh, 0.0)
        return decay * factor, scale(factor, state) + fresh

    apart = ((3, from3), (2, from2), (1, from1))
    for d, ref in apart:
        decay, state = follow(decay, state, ref, zl >= d)
    state_before[...] = state
    decay_before[...] = decay
    factor, fresh = unpack(own)
    decay, state = decay * factor, scale(factor, state) + fresh
    for d, ref in apart:
        decay, state = follow(decay, state, ref, zl < d)
    pack(total, decay, state)


def whole_kernel(
    meta, from1, from2, from3, state_before, decay_before, state_first, decay_first, out, keep
):
    core = meta[1]
    state = jnp.zeros((STATE_ROWS, STATE), f32)
    for ref in (from3, from2, from1):
        factor, fresh = unpack(ref)
        state = scale(factor, state) + fresh
    entering = scale(decay_before[...], state) + state_before[...]
    second = scale(decay_first[...], entering) + state_first[...]
    out[...] = jnp.where(core == 0, second, entering).astype(bf16)
    keep[...] = jnp.where(core == 0, entering, second).astype(bf16)


def inside_kernel(
    meta, decay_logs, skip_scale, x, writes, reads, steps, gates, early, late
):
    first = meta[0]
    rates = jnp.exp(head_rows(decay_logs))
    row = lax.broadcasted_iota(jnp.int32, (SPAN, SPAN), 0)
    col = lax.broadcasted_iota(jnp.int32, (SPAN, SPAN), 1)
    upto = jnp.where(row <= col, 1.0, 0.0).astype(f32)
    below = jnp.where(row >= col, 1.0, 0.0).astype(f32)
    for p in range(PAIRS):
        limit = meta[2 + p]
        step = steps[p]
        drop = -rates * step
        cumul = jnp.dot(drop, upto, precision=EXACT, preferred_element_type=f32)
        turned = lax.dot_general(
            below, drop, (((1,), (1,)), ((), ())), precision=EXACT, preferred_element_type=f32
        )
        part_row = jnp.where(first + row >= limit, 1, 0)
        part_col = jnp.where(first + col >= limit, 1, 0)
        previous = jnp.where(first - 1 >= limit, 1, 0)
        allowed = (part_row == part_col) & (row >= col)
        scores = lax.dot_general(
            reads[p], writes[p], (((1,), (1,)), ((), ())), preferred_element_type=f32
        )
        scores = jnp.where(allowed, scores, 0.0)
        reached = jnp.where(part_row[:, :CHANNELS] == previous, 1.0, 0.0)
        for h in range(HEADS_LOCAL):
            here = slice(h * CHANNELS, (h + 1) * CHANNELS)
            column = turned[:, h : h + 1]
            decay = jnp.exp(jnp.minimum(column - cumul[h : h + 1, :], 0.0))
            weights = (scores * decay * step[h : h + 1, :]).astype(bf16)
            inputs = x[p, :, here]
            intra = jnp.dot(weights, inputs, preferred_element_type=f32)
            ssm = intra + skip_scale[h] * inputs.astype(f32)
            gate = gates[p, :, here].astype(f32)
            opened = gate / (1.0 + jnp.exp(-gate))
            early[p, :, here] = ssm * opened
            late[p, :, here] = opened * reached * jnp.exp(column)


def scaled_kernel(weight, gain, out):
    row = lax.broadcasted_iota(jnp.int32, (SPAN, SPAN), 0)
    col = lax.broadcasted_iota(jnp.int32, (SPAN, SPAN), 1)
    for part in range(WIDTH // SPAN):
        here = pl.ds(part * SPAN, SPAN)
        gains = jnp.broadcast_to(gain[:, part * SPAN : (part + 1) * SPAN], (SPAN, SPAN))
        turned = jnp.sum(jnp.where(row == col, gains, 0.0), axis=1, keepdims=True)
        out[here, :] = (weight[here, :].astype(f32) * turned).astype(bf16)


def hidden_kernel(meta, keep, got, reads, early, late, *outs):
    core = meta[1]
    rows = HALF * CHANNELS
    for p, out in enumerate(outs):
        here = pl.ds(p * rows, rows)
        own, other = keep[here, :], got[here, :]
        for half in range(2):
            state = jnp.where(core == half, own, other)
            columns = slice(half * rows, (half + 1) * rows)
            carry = lax.dot_general(
                reads[p], state, (((1,), (1,)), ((), ())), preferred_element_type=f32
            )
            gated = early[p, :, columns] + late[p, :, columns] * carry
            out[:, columns] = gated.astype(bf16)


def arrange_kernel(meta, spot, *refs):
    chunks, hidden, tails = refs[: PAIRS * NZH], refs[-2], refs[-1]
    zh = meta[5]
    ones = jnp.ones((8, WIDTH), f32)
    for p in range(PAIRS):
        here = pl.ds(p * SPAN, SPAN)
        total = jnp.zeros((SPAN, WIDTH), f32)
        for k, move in enumerate((0, NZH - 1, 1, 2)):
            chunk = chunks[PAIRS * k + p][...]
            turn = spot[zh * NZH + (zh + move) % NZH]
            columns = pl.ds(pl.multiple_of(turn * WIDTH, WIDTH), WIDTH)
            hidden[here, columns] = chunk
            wide = chunk.astype(f32)
            total += wide * wide
        squares = lax.dot_general(
            ones, total, (((1,), (1,)), ((), ())), precision=EXACT, preferred_element_type=f32
        )
        high = squares.astype(bf16).astype(f32)
        for place, part in ((p * SPAN, high), (TOKENS + p * SPAN, squares - high)):
            tails[:, pl.ds(place, SPAN)] = jnp.concatenate([part, part], axis=0).astype(bf16)


def project_kernel(meta, hidden, tails, weight, *refs):
    outs, here, sem = refs[:NY], refs[NY], refs[NY + 1]
    half = WIDTH // 2
    order = [(d, core) for d in (2, 1, 3, 0) for core in range(NCORE)]
    copies = []
    for slot, (d, core) in enumerate(order):
        copy = pltpu.make_async_copy(
            weight.at[(meta[6] + d) % NY, core], here.at[slot], sem.at[slot]
        )
        copy.start()
        copies.append(copy)
    for out in outs:
        out[pl.ds(TOKENS, 16), :] = tails[...]
    for slot, (d, core) in enumerate(order):
        copies[slot].wait()
        total = jnp.dot(hidden[...], here[slot], preferred_element_type=f32)
        outs[d][pl.ds(0, TOKENS), pl.ds(core * half, half)] = total.astype(bf16)


def finish_kernel(own, got1, got2, got3, out):
    refs = (own, got1, got2, got3)
    row = lax.broadcasted_iota(jnp.int32, (SPAN, SPAN), 0)
    col = lax.broadcasted_iota(jnp.int32, (SPAN, SPAN), 1)
    for p in range(PAIRS):
        here = pl.ds(p * SPAN, SPAN)
        squares = jnp.zeros((16, SPAN), f32)
        for ref in refs:
            squares += ref[pl.ds(TOKENS, 16), pl.ds(p * SPAN, SPAN)].astype(f32)
            squares += ref[pl.ds(TOKENS, 16), pl.ds(TOKENS + p * SPAN, SPAN)].astype(f32)
        factor = lax.rsqrt(squares / INNER + EPSILON)
        spread = jnp.broadcast_to(factor[:1], (SPAN, SPAN))
        turned = jnp.sum(jnp.where(row == col, spread, 0.0), axis=1, keepdims=True)
        total = sum(ref[here, :].astype(f32) for ref in refs)
        out[p] = (total * turned).astype(bf16)


def finish_kernel(own, got1, got2, got3, out):
    refs = (own, got1, got2, got3)
    squares = jnp.zeros((16, TOKENS), f32)
    for ref in refs:
        tail = ref[pl.ds(TOKENS, 16), :].astype(f32)
        squares += tail[:, :TOKENS] + tail[:, TOKENS:]
    factor = lax.rsqrt(squares[:8] / INNER + EPSILON)
    row = lax.broadcasted_iota(jnp.int32, (SPAN, SPAN), 0)
    col = lax.broadcasted_iota(jnp.int32, (SPAN, SPAN), 1)
    same = jnp.where(row == col, 1.0, 0.0).astype(f32)
    for p in range(PAIRS):
        here = pl.ds(p * SPAN, SPAN)
        turned = lax.dot_general(
            same,
            factor[:, p * SPAN : (p + 1) * SPAN],
            (((1,), (1,)), ((), ())),
            precision=EXACT,
            preferred_element_type=f32,
        )
        total = sum(ref[here, :].astype(f32) for ref in refs)
        out[p] = (total * turned[:, :1]).astype(bf16)


def shards(
    head_inputs,
    gate_inputs,
    write_vectors,
    read_vectors,
    step_sizes,
    decay_logs,
    skip_scale,
    norm_gain,
    out_weight,
    boundary,
):
    seq, head = lax.axis_index("seq"), lax.axis_index("head")
    zl, core = (seq // NCORE) % NZL, seq % NCORE
    y, zh = head // NZH, head % NZH
    first = seq * SPAN
    meta = jnp.concatenate(
        [jnp.stack([first, core]).astype(jnp.int32), boundary, jnp.stack([zl, zh, y]).astype(jnp.int32)]
    )

    group = head // 2
    writes = lax.dynamic_index_in_dim(write_vectors, group, 2, keepdims=False)
    reads = lax.dynamic_index_in_dim(read_vectors, group, 2, keepdims=False)

    payload = shape((PAYLOAD_ROWS, STATE), bf16)
    wide = shape((STATE_ROWS, STATE), f32)
    small = shape((PAIRS * HALF, STATE), f32)
    scaled = call(
        scaled_kernel,
        shape((WIDTH, WIDTH // 2), bf16),
        [VMEM, VMEM],
        (out_weight, norm_gain.reshape(1, WIDTH)),
        2**18,
        2**19,
    )
    near = swap_z(scaled)
    leaving, mine, decay_mine = call(
        states_kernel,
        (payload, wide, small),
        [SMEM, SMEM, VMEM, VMEM, VMEM],
        (meta, decay_logs, head_inputs, writes, step_sizes),
        2 * 2**24,
        2**20,
    )
    total, state_first, decay_first = call(
        chip_kernel,
        (payload, wide, small),
        [SMEM, VMEM, VMEM, VMEM],
        (meta, to_core(leaving), mine, decay_mine),
        2**18,
        2**19,
    )
    local = shape((PAIRS, SPAN, WIDTH), f32)
    early, late = call(
        inside_kernel,
        (local, local),
        [SMEM, SMEM, SMEM] + [VMEM] * 5,
        (meta, decay_logs, skip_scale, head_inputs, writes, reads, step_sizes, gate_inputs),
        2**26,
        2**21,
    )
    near, total = lax.optimization_barrier((near, total))
    from_zl = [to_zl(total, d) for d in (1, 2, 3)]
    early, *from_zl = lax.optimization_barrier((early, *from_zl))
    line, state_before, decay_before = call(
        line_kernel,
        (payload, wide, small),
        [SMEM] + [VMEM] * 4,
        (meta, total, *from_zl),
        2**18,
        2**19,
    )
    from_x = [to_x(line, d) for d in (1, 2, 3)]
    half_state = shape((STATE_ROWS, STATE), bf16)
    crossing, keep = call(
        whole_kernel,
        (half_state, half_state),
        [SMEM] + [VMEM] * 7,
        (meta, *from_x)
        + (state_before, decay_before, state_first, decay_first),
        2**18,
        2**19,
    )
    got = to_core(crossing)

    token_part = shape((SPAN, WIDTH), bf16)
    first, second = call(
        hidden_kernel,
        (token_part, token_part),
        [SMEM] + [VMEM] * 5,
        (meta, keep, got, reads, early, late),
        2**25,
        2**21,
    )
    line_weight = gather(near, lambda x, zl, core: (x, core))
    line_weight, first, second = lax.optimization_barrier((line_weight, first, second))
    weight = gather(line_weight, lambda x, zl, core: zl)
    weight = weight.reshape(NX, NCORE, NZH * WIDTH, WIDTH // 2)

    first_below, second_above = to_zh(first, 1), to_zh(second, NZH - 1)
    second_below, first_above = to_zh(second, 1), to_zh(first, NZH - 1)
    far = (to_zh(first_below, 1), to_zh(second_above, NZH - 1))
    chunks = (first, second, first_below, second_below, first_above, second_above) + far
    places = jnp.array(SPOT, jnp.int32).reshape(-1)
    arranged, tails = call(
        arrange_kernel,
        (shape((TOKENS, NZH * WIDTH), bf16), shape((16, WIDTH), bf16)),
        [SMEM, SMEM] + [VMEM] * PAIRS * NZH,
        (meta, places, *chunks),
        2**24,
        2**21,
    )
    partial = shape((TOKEN_ROWS, WIDTH), bf16)
    blocks = NY * NCORE
    partials = call(
        project_kernel,
        (partial,) * NY,
        [SMEM, VMEM, VMEM, pl.BlockSpec(memory_space=pl.ANY)],
        (meta, arranged, tails, weight),
        2**31,
        2**23,
        [
            pltpu.VMEM((blocks, NZH * WIDTH, WIDTH // 2), bf16),
            pltpu.SemaphoreType.DMA((blocks,)),
        ],
        58 * 2**20,
    )
    arrived = [to_y(partials[d], d) for d in (2, 1, 3)]
    return call(
        finish_kernel,
        shape((PAIRS, SPAN, WIDTH), bf16),
        [VMEM] * 4,
        (partials[0], *arrived),
        2**20,
        2**20,
    )


def solution(mesh):
    return jax.shard_map(
        shards,
        mesh=mesh,
        in_specs=(
            P(None, "seq", "head"),
            P(None, "seq", "head"),
            P(None, "seq", None, None),
            P(None, "seq", None, None),
            P(None, "head", "seq"),
            P("head"),
            P("head"),
            P("head"),
            P("head", "seq"),
            P(),
        ),
        out_specs=P(None, "seq", "head"),
        check_vma=False,
    )
```

```python
import jax
import jax.numpy as jnp
from jax import lax
from jax.experimental import pallas as pl
from jax.experimental.pallas import tpu as pltpu
from jax.sharding import PartitionSpec as P

INNER = 8192
EPSILON = 1e-05
PAIRS = 2
SPAN = 128
HEADS_LOCAL = 8
HALF = 4
CHANNELS = 64
STATE = 128
WIDTH = 512
TOKENS = PAIRS * SPAN
STATE_ROWS = PAIRS * HALF * CHANNELS
PAYLOAD_ROWS = STATE_ROWS + 16
SPOT = ((0, 2, 3, 1), (1, 2, 3, 0), (3, 0, 1, 2), (2, 0, 1, 3))
TOKEN_ROWS = TOKENS + 16
NX = NZL = NY = NZH = 4
NCORE = 2
EXACT = lax.Precision.HIGHEST
f32 = jnp.float32
bf16 = jnp.bfloat16


def seq_index(x, zl, core):
    return (x * NZL + zl) * NCORE + core


def head_index(y, zh):
    return y * NZH + zh


def route(move):
    pairs = []
    for x in range(NX):
        for zl in range(NZL):
            for core in range(NCORE):
                for y in range(NY):
                    for zh in range(NZH):
                        to = move(x, zl, core, y, zh)
                        if to is None:
                            continue
                        source = seq_index(x, zl, core) * NY * NZH + head_index(y, zh)
                        target = seq_index(*to[:3]) * NY * NZH + head_index(*to[3:])
                        pairs.append((source, target))
    return pairs


def send(value, move):
    return lax.ppermute(value, ("seq", "head"), route(move))


def to_core(value):
    return send(value, lambda x, zl, c, y, zh: (x, zl, 1 - c, y, zh))


def to_zl(value, d):
    return send(value, lambda x, zl, c, y, zh: (x, (zl + d) % NZL, c, y, zh))


def to_x(value, d):
    return send(value, lambda x, zl, c, y, zh: (x + d, zl, c, y, zh) if x + d < NX else None)


def to_y(value, d):
    return send(value, lambda x, zl, c, y, zh: (x, zl, c, (y + d) % NY, zh))


def to_zh(value, d):
    return send(value, lambda x, zl, c, y, zh: (x, zl, c, y, (zh + d) % NZH))


def swap_z(value):
    return send(value, lambda x, zl, c, y, zh: (x, SPOT[zl][zh], c, y, zl))


def gather(block, key):
    groups = {}
    for x in range(NX):
        for zl in range(NZL):
            for core in range(NCORE):
                groups.setdefault(key(x, zl, core), []).append(seq_index(x, zl, core))
    return lax.all_gather(
        block, "seq", axis=0, tiled=True, axis_index_groups=list(groups.values())
    )


VMEM = pl.BlockSpec(memory_space=pltpu.VMEM)
SMEM = pl.BlockSpec(memory_space=pltpu.SMEM)


def call(kernel, outs, specs, args, flops, moved, scratch=(), limit=16 * 2**20):
    return pl.pallas_call(
        kernel,
        out_shape=outs,
        in_specs=specs,
        out_specs=jax.tree.map(lambda _: VMEM, outs),
        scratch_shapes=scratch,
        cost_estimate=pl.CostEstimate(flops=flops, bytes_accessed=moved, transcendentals=0),
        compiler_params=pltpu.CompilerParams(vmem_limit_bytes=limit),
    )(*args)


def shape(dims, kind):
    return jax.ShapeDtypeStruct(dims, kind)


def head_rows(scalars):
    rows = lax.broadcasted_iota(jnp.int32, (HEADS_LOCAL, SPAN), 0)
    out = jnp.zeros((HEADS_LOCAL, SPAN), f32)
    for h in range(HEADS_LOCAL):
        out = jnp.where(rows == h, scalars[h], out)
    return out


def states_kernel(meta, decay_logs, x, writes, steps, out, mine, decay_mine):
    first, core = meta[0], meta[1]
    rates = jnp.exp(head_rows(decay_logs))
    row = lax.broadcasted_iota(jnp.int32, (SPAN, SPAN), 0)
    col = lax.broadcasted_iota(jnp.int32, (SPAN, SPAN), 1)
    upto = jnp.where(row <= col, 1.0, 0.0).astype(f32)
    position = first + lax.broadcasted_iota(jnp.int32, (HEADS_LOCAL, SPAN), 1)
    send_decay, keep_decay = [], []
    rows = HALF * CHANNELS
    for p in range(PAIRS):
        limit = meta[2 + p]
        step = steps[p]
        cumul = jnp.dot(-rates * step, upto, precision=EXACT, preferred_element_type=f32)
        last = cumul[:, SPAN - 1 :]
        last_part = jnp.where(first + SPAN - 1 >= limit, 1, 0)
        previous = jnp.where(first - 1 >= limit, 1, 0)
        part = jnp.where(position >= limit, 1, 0)
        ends = jnp.exp(last - cumul) * step
        ends = jnp.where(part == last_part, ends, 0.0)
        spread = jnp.broadcast_to(ends[:, None, :], (HEADS_LOCAL, CHANNELS, SPAN))
        spread = spread.reshape(HEADS_LOCAL * CHANNELS, SPAN)
        turned = x[p].astype(f32).T
        state = jnp.dot(
            (turned * spread).astype(bf16), writes[p], preferred_element_type=f32
        )
        passing = jnp.broadcast_to(jnp.exp(last), (HEADS_LOCAL, SPAN))
        passing = jnp.where(last_part == previous, passing, 0.0)
        here = pl.ds(p * rows, rows)
        lower, upper = state[:rows], state[rows:]
        out[here, :] = jnp.where(core == 0, upper, lower).astype(bf16)
        mine[here, :] = jnp.where(core == 0, lower, upper)
        send_decay.append(jnp.where(core == 0, passing[HALF:], passing[:HALF]))
        keep_decay.append(jnp.where(core == 0, passing[:HALF], passing[HALF:]))
    leaving = jnp.concatenate(send_decay, axis=0)
    high = leaving.astype(bf16).astype(f32)
    out[pl.ds(STATE_ROWS, 16), :] = jnp.concatenate([high, leaving - high], axis=0).astype(bf16)
    decay_mine[...] = jnp.concatenate(keep_decay, axis=0)


def unpack(ref):
    tail = ref[pl.ds(STATE_ROWS, 16), :].astype(f32)
    return tail[:8] + tail[8:], ref[pl.ds(0, STATE_ROWS), :].astype(f32)


def scale(decay, state):
    groups = PAIRS * HALF
    return (state.reshape(groups, CHANNELS, STATE) * decay[:, None, :]).reshape(STATE_ROWS, STATE)


def pack(out, decay, state):
    out[pl.ds(0, STATE_ROWS), :] = state.astype(bf16)
    high = decay.astype(bf16).astype(f32)
    out[pl.ds(STATE_ROWS, 16), :] = jnp.concatenate([high, decay - high], axis=0).astype(bf16)


def chip_kernel(meta, got, mine, decay_mine, total, state_first, decay_first):
    core = meta[1]
    decay_got, state_got = unpack(got)
    decay_own, state_own = decay_mine[...], mine[...]
    decay0 = jnp.where(core == 0, decay_own, decay_got)
    decay1 = jnp.where(core == 0, decay_got, decay_own)
    state0 = jnp.where(core == 0, state_own, state_got)
    state1 = jnp.where(core == 0, state_got, state_own)
    state_first[...] = state0
    decay_first[...] = decay0
    pack(total, decay0 * decay1, scale(decay1, state0) + state1)


def line_kernel(meta, own, from1, from2, from3, total, state_before, decay_before):
    zl = meta[4]
    state = jnp.zeros((STATE_ROWS, STATE), f32)
    decay = jnp.ones((PAIRS * HALF, STATE), f32)

    def follow(decay, state, ref, valid):
        factor, fresh = unpack(ref)
        factor = jnp.where(valid, factor, 1.0)
        fresh = jnp.where(valid, fresh, 0.0)
        return decay * factor, scale(factor, state) + fresh

    apart = ((3, from3), (2, from2), (1, from1))
    for d, ref in apart:
        decay, state = follow(decay, state, ref, zl >= d)
    state_before[...] = state
    decay_before[...] = decay
    factor, fresh = unpack(own)
    decay, state = decay * factor, scale(factor, state) + fresh
    for d, ref in apart:
        decay, state = follow(decay, state, ref, zl < d)
    pack(total, decay, state)


def whole_kernel(
    meta, from1, from2, from3, state_before, decay_before, state_first, decay_first, out, keep
):
    core = meta[1]
    state = jnp.zeros((STATE_ROWS, STATE), f32)
    for ref in (from3, from2, from1):
        factor, fresh = unpack(ref)
        state = scale(factor, state) + fresh
    entering = scale(decay_before[...], state) + state_before[...]
    second = scale(decay_first[...], entering) + state_first[...]
    out[...] = jnp.where(core == 0, second, entering).astype(bf16)
    keep[...] = jnp.where(core == 0, entering, second).astype(bf16)


def inside_kernel(
    meta, decay_logs, skip_scale, x, writes, reads, steps, gates, early, late
):
    first = meta[0]
    rates = jnp.exp(head_rows(decay_logs))
    row = lax.broadcasted_iota(jnp.int32, (SPAN, SPAN), 0)
    col = lax.broadcasted_iota(jnp.int32, (SPAN, SPAN), 1)
    upto = jnp.where(row <= col, 1.0, 0.0).astype(f32)
    below = jnp.where(row >= col, 1.0, 0.0).astype(f32)
    for p in range(PAIRS):
        limit = meta[2 + p]
        step = steps[p]
        drop = -rates * step
        cumul = jnp.dot(drop, upto, precision=EXACT, preferred_element_type=f32)
        turned = lax.dot_general(
            below, drop, (((1,), (1,)), ((), ())), precision=EXACT, preferred_element_type=f32
        )
        part_row = jnp.where(first + row >= limit, 1, 0)
        part_col = jnp.where(first + col >= limit, 1, 0)
        previous = jnp.where(first - 1 >= limit, 1, 0)
        allowed = (part_row == part_col) & (row >= col)
        scores = lax.dot_general(
            reads[p], writes[p], (((1,), (1,)), ((), ())), preferred_element_type=f32
        )
        scores = jnp.where(allowed, scores, 0.0)
        reached = jnp.where(part_row[:, :CHANNELS] == previous, 1.0, 0.0)
        for h in range(HEADS_LOCAL):
            here = slice(h * CHANNELS, (h + 1) * CHANNELS)
            column = turned[:, h : h + 1]
            decay = jnp.exp(jnp.minimum(column - cumul[h : h + 1, :], 0.0))
            weights = (scores * decay * step[h : h + 1, :]).astype(bf16)
            inputs = x[p, :, here]
            intra = jnp.dot(weights, inputs, preferred_element_type=f32)
            ssm = intra + skip_scale[h] * inputs.astype(f32)
            gate = gates[p, :, here].astype(f32)
            opened = gate / (1.0 + jnp.exp(-gate))
            early[p, :, here] = ssm * opened
            late[p, :, here] = opened * reached * jnp.exp(column)


def scaled_kernel(weight, gain, out):
    row = lax.broadcasted_iota(jnp.int32, (SPAN, SPAN), 0)
    col = lax.broadcasted_iota(jnp.int32, (SPAN, SPAN), 1)
    for part in range(WIDTH // SPAN):
        here = pl.ds(part * SPAN, SPAN)
        gains = jnp.broadcast_to(gain[:, part * SPAN : (part + 1) * SPAN], (SPAN, SPAN))
        turned = jnp.sum(jnp.where(row == col, gains, 0.0), axis=1, keepdims=True)
        out[here, :] = (weight[here, :].astype(f32) * turned).astype(bf16)


def hidden_kernel(meta, keep, got, reads, early, late, *outs):
    core = meta[1]
    rows = HALF * CHANNELS
    for p, out in enumerate(outs):
        here = pl.ds(p * rows, rows)
        own, other = keep[here, :], got[here, :]
        for half in range(2):
            state = jnp.where(core == half, own, other)
            columns = slice(half * rows, (half + 1) * rows)
            carry = lax.dot_general(
                reads[p], state, (((1,), (1,)), ((), ())), preferred_element_type=f32
            )
            gated = early[p, :, columns] + late[p, :, columns] * carry
            out[:, columns] = gated.astype(bf16)


def arrange_kernel(meta, spot, *refs):
    chunks, hidden, tails = refs[: PAIRS * NZH], refs[-2], refs[-1]
    zh = meta[5]
    ones = jnp.ones((8, WIDTH), f32)
    for p in range(PAIRS):
        here = pl.ds(p * SPAN, SPAN)
        total = jnp.zeros((SPAN, WIDTH), f32)
        for k, move in enumerate((0, NZH - 1, 1, 2)):
            chunk = chunks[PAIRS * k + p][...]
            turn = spot[zh * NZH + (zh + move) % NZH]
            columns = pl.ds(pl.multiple_of(turn * WIDTH, WIDTH), WIDTH)
            hidden[here, columns] = chunk
            wide = chunk.astype(f32)
            total += wide * wide
        squares = lax.dot_general(
            ones, total, (((1,), (1,)), ((), ())), precision=EXACT, preferred_element_type=f32
        )
        high = squares.astype(bf16).astype(f32)
        for place, part in ((p * SPAN, high), (TOKENS + p * SPAN, squares - high)):
            tails[:, pl.ds(place, SPAN)] = jnp.concatenate([part, part], axis=0).astype(bf16)


def project_kernel(index, hidden, tails, weight, out):
    half = WIDTH // 2
    for core in range(NCORE):
        total = jnp.dot(hidden[...], weight[index[0], core], preferred_element_type=f32)
        out[pl.ds(0, TOKENS), pl.ds(core * half, half)] = total.astype(bf16)
    out[pl.ds(TOKENS, 16), :] = tails[...]


def finish_kernel(own, got1, got2, got3, out):
    refs = (own, got1, got2, got3)
    row = lax.broadcasted_iota(jnp.int32, (SPAN, SPAN), 0)
    col = lax.broadcasted_iota(jnp.int32, (SPAN, SPAN), 1)
    for p in range(PAIRS):
        here = pl.ds(p * SPAN, SPAN)
        squares = jnp.zeros((16, SPAN), f32)
        for ref in refs:
            squares += ref[pl.ds(TOKENS, 16), pl.ds(p * SPAN, SPAN)].astype(f32)
            squares += ref[pl.ds(TOKENS, 16), pl.ds(TOKENS + p * SPAN, SPAN)].astype(f32)
        factor = lax.rsqrt(squares / INNER + EPSILON)
        spread = jnp.broadcast_to(factor[:1], (SPAN, SPAN))
        turned = jnp.sum(jnp.where(row == col, spread, 0.0), axis=1, keepdims=True)
        total = sum(ref[here, :].astype(f32) for ref in refs)
        out[p] = (total * turned).astype(bf16)


def finish_kernel(own, got1, got2, got3, out):
    refs = (own, got1, got2, got3)
    squares = jnp.zeros((16, TOKENS), f32)
    for ref in refs:
        tail = ref[pl.ds(TOKENS, 16), :].astype(f32)
        squares += tail[:, :TOKENS] + tail[:, TOKENS:]
    factor = lax.rsqrt(squares[:8] / INNER + EPSILON)
    row = lax.broadcasted_iota(jnp.int32, (SPAN, SPAN), 0)
    col = lax.broadcasted_iota(jnp.int32, (SPAN, SPAN), 1)
    same = jnp.where(row == col, 1.0, 0.0).astype(f32)
    for p in range(PAIRS):
        here = pl.ds(p * SPAN, SPAN)
        turned = lax.dot_general(
            same,
            factor[:, p * SPAN : (p + 1) * SPAN],
            (((1,), (1,)), ((), ())),
            precision=EXACT,
            preferred_element_type=f32,
        )
        total = sum(ref[here, :].astype(f32) for ref in refs)
        out[p] = (total * turned[:, :1]).astype(bf16)


def shards(
    head_inputs,
    gate_inputs,
    write_vectors,
    read_vectors,
    step_sizes,
    decay_logs,
    skip_scale,
    norm_gain,
    out_weight,
    boundary,
):
    seq, head = lax.axis_index("seq"), lax.axis_index("head")
    zl, core = (seq // NCORE) % NZL, seq % NCORE
    y, zh = head // NZH, head % NZH
    first = seq * SPAN
    meta = jnp.concatenate(
        [jnp.stack([first, core]).astype(jnp.int32), boundary, jnp.stack([zl, zh, y]).astype(jnp.int32)]
    )

    group = head // 2
    writes = lax.dynamic_index_in_dim(write_vectors, group, 2, keepdims=False)
    reads = lax.dynamic_index_in_dim(read_vectors, group, 2, keepdims=False)

    payload = shape((PAYLOAD_ROWS, STATE), bf16)
    wide = shape((STATE_ROWS, STATE), f32)
    small = shape((PAIRS * HALF, STATE), f32)
    scaled = call(
        scaled_kernel,
        shape((WIDTH, WIDTH // 2), bf16),
        [VMEM, VMEM],
        (out_weight, norm_gain.reshape(1, WIDTH)),
        2**18,
        2**19,
    )
    near = swap_z(scaled)
    leaving, mine, decay_mine = call(
        states_kernel,
        (payload, wide, small),
        [SMEM, SMEM, VMEM, VMEM, VMEM],
        (meta, decay_logs, head_inputs, writes, step_sizes),
        2 * 2**24,
        2**20,
    )
    total, state_first, decay_first = call(
        chip_kernel,
        (payload, wide, small),
        [SMEM, VMEM, VMEM, VMEM],
        (meta, to_core(leaving), mine, decay_mine),
        2**18,
        2**19,
    )
    local = shape((PAIRS, SPAN, WIDTH), f32)
    early, late = call(
        inside_kernel,
        (local, local),
        [SMEM, SMEM, SMEM] + [VMEM] * 5,
        (meta, decay_logs, skip_scale, head_inputs, writes, reads, step_sizes, gate_inputs),
        2**26,
        2**21,
    )
    near, total = lax.optimization_barrier((near, total))
    from_zl = [to_zl(total, d) for d in (1, 2, 3)]
    early, *from_zl = lax.optimization_barrier((early, *from_zl))
    line, state_before, decay_before = call(
        line_kernel,
        (payload, wide, small),
        [SMEM] + [VMEM] * 4,
        (meta, total, *from_zl),
        2**18,
        2**19,
    )
    from_x = [to_x(line, d) for d in (1, 2, 3)]
    half_state = shape((STATE_ROWS, STATE), bf16)
    crossing, keep = call(
        whole_kernel,
        (half_state, half_state),
        [SMEM] + [VMEM] * 7,
        (meta, *from_x)
        + (state_before, decay_before, state_first, decay_first),
        2**18,
        2**19,
    )
    got = to_core(crossing)

    token_part = shape((SPAN, WIDTH), bf16)
    first, second = call(
        hidden_kernel,
        (token_part, token_part),
        [SMEM] + [VMEM] * 5,
        (meta, keep, got, reads, early, late),
        2**25,
        2**21,
    )
    line_weight = gather(near, lambda x, zl, core: (x, core))
    line_weight, first, second = lax.optimization_barrier((line_weight, first, second))
    weight = gather(line_weight, lambda x, zl, core: zl)
    weight = weight.reshape(NX, NCORE, NZH * WIDTH, WIDTH // 2)

    first_below, second_above = to_zh(first, 1), to_zh(second, NZH - 1)
    second_below, first_above = to_zh(second, 1), to_zh(first, NZH - 1)
    far = (to_zh(first_below, 1), to_zh(second_above, NZH - 1))
    chunks = (first, second, first_below, second_below, first_above, second_above) + far
    places = jnp.array(SPOT, jnp.int32).reshape(-1)
    arranged, tails = call(
        arrange_kernel,
        (shape((TOKENS, NZH * WIDTH), bf16), shape((16, WIDTH), bf16)),
        [SMEM, SMEM] + [VMEM] * PAIRS * NZH,
        (meta, places, *chunks),
        2**24,
        2**21,
    )
    def partial(d):
        return call(
            project_kernel,
            shape((TOKEN_ROWS, WIDTH), bf16),
            [SMEM] + [VMEM] * 3,
            (((y + d) % NY).reshape(1), arranged, tails, weight),
            2**29,
            2**21,
            (),
            24 * 2**20,
        )

    arrived = [to_y(partial(d), d) for d in (2, 1, 3)]
    return call(
        finish_kernel,
        shape((PAIRS, SPAN, WIDTH), bf16),
        [VMEM] * 4,
        (partial(0), *arrived),
        2**20,
        2**20,
    )


def solution(mesh):
    return jax.shard_map(
        shards,
        mesh=mesh,
        in_specs=(
            P(None, "seq", "head"),
            P(None, "seq", "head"),
            P(None, "seq", None, None),
            P(None, "seq", None, None),
            P(None, "head", "seq"),
            P("head"),
            P("head"),
            P("head"),
            P("head", "seq"),
            P(),
        ),
        out_specs=P(None, "seq", "head"),
        check_vma=False,
    )
```

```python
import jax
import jax.numpy as jnp
from jax import lax
from jax.experimental import pallas as pl
from jax.experimental.pallas import tpu as pltpu
from jax.sharding import PartitionSpec as P

INNER = 8192
EPSILON = 1e-05
PAIRS = 2
SPAN = 128
HEADS_LOCAL = 8
HALF = 4
CHANNELS = 64
STATE = 128
WIDTH = 512
TOKENS = PAIRS * SPAN
STATE_ROWS = PAIRS * HALF * CHANNELS
PAYLOAD_ROWS = STATE_ROWS + 16
SPOT = ((0, 2, 3, 1), (1, 2, 3, 0), (3, 0, 1, 2), (2, 0, 1, 3))
TOKEN_ROWS = TOKENS + 16
NX = NZL = NY = NZH = 4
NCORE = 2
EXACT = lax.Precision.HIGHEST
f32 = jnp.float32
bf16 = jnp.bfloat16


def seq_index(x, zl, core):
    return (x * NZL + zl) * NCORE + core


def head_index(y, zh):
    return y * NZH + zh


def route(move):
    pairs = []
    for x in range(NX):
        for zl in range(NZL):
            for core in range(NCORE):
                for y in range(NY):
                    for zh in range(NZH):
                        to = move(x, zl, core, y, zh)
                        if to is None:
                            continue
                        source = seq_index(x, zl, core) * NY * NZH + head_index(y, zh)
                        target = seq_index(*to[:3]) * NY * NZH + head_index(*to[3:])
                        pairs.append((source, target))
    return pairs


def send(value, move):
    return lax.ppermute(value, ("seq", "head"), route(move))


def to_core(value):
    return send(value, lambda x, zl, c, y, zh: (x, zl, 1 - c, y, zh))


def to_zl(value, d):
    return send(value, lambda x, zl, c, y, zh: (x, (zl + d) % NZL, c, y, zh))


def to_x(value, d):
    return send(value, lambda x, zl, c, y, zh: (x + d, zl, c, y, zh) if x + d < NX else None)


def to_y(value, d):
    return send(value, lambda x, zl, c, y, zh: (x, zl, c, (y + d) % NY, zh))


def to_zh(value, d):
    return send(value, lambda x, zl, c, y, zh: (x, zl, c, y, (zh + d) % NZH))


def swap_z(value):
    return send(value, lambda x, zl, c, y, zh: (x, SPOT[zl][zh], c, y, zl))


def gather(block, key):
    groups = {}
    for x in range(NX):
        for zl in range(NZL):
            for core in range(NCORE):
                groups.setdefault(key(x, zl, core), []).append(seq_index(x, zl, core))
    return lax.all_gather(
        block, "seq", axis=0, tiled=True, axis_index_groups=list(groups.values())
    )


VMEM = pl.BlockSpec(memory_space=pltpu.VMEM)
SMEM = pl.BlockSpec(memory_space=pltpu.SMEM)


def call(kernel, outs, specs, args, flops, moved, scratch=(), limit=16 * 2**20):
    return pl.pallas_call(
        kernel,
        out_shape=outs,
        in_specs=specs,
        out_specs=jax.tree.map(lambda _: VMEM, outs),
        scratch_shapes=scratch,
        cost_estimate=pl.CostEstimate(flops=flops, bytes_accessed=moved, transcendentals=0),
        compiler_params=pltpu.CompilerParams(vmem_limit_bytes=limit),
    )(*args)


def shape(dims, kind):
    return jax.ShapeDtypeStruct(dims, kind)


def head_rows(scalars):
    rows = lax.broadcasted_iota(jnp.int32, (HEADS_LOCAL, SPAN), 0)
    out = jnp.zeros((HEADS_LOCAL, SPAN), f32)
    for h in range(HEADS_LOCAL):
        out = jnp.where(rows == h, scalars[h], out)
    return out


def states_kernel(meta, decay_logs, x, writes, steps, out, mine, decay_mine):
    first, core = meta[0], meta[1]
    rates = jnp.exp(head_rows(decay_logs))
    row = lax.broadcasted_iota(jnp.int32, (SPAN, SPAN), 0)
    col = lax.broadcasted_iota(jnp.int32, (SPAN, SPAN), 1)
    upto = jnp.where(row <= col, 1.0, 0.0).astype(f32)
    position = first + lax.broadcasted_iota(jnp.int32, (HEADS_LOCAL, SPAN), 1)
    send_decay, keep_decay = [], []
    rows = HALF * CHANNELS
    for p in range(PAIRS):
        limit = meta[2 + p]
        step = steps[p]
        cumul = jnp.dot(-rates * step, upto, precision=EXACT, preferred_element_type=f32)
        last = cumul[:, SPAN - 1 :]
        last_part = jnp.where(first + SPAN - 1 >= limit, 1, 0)
        previous = jnp.where(first - 1 >= limit, 1, 0)
        part = jnp.where(position >= limit, 1, 0)
        ends = jnp.exp(last - cumul) * step
        ends = jnp.where(part == last_part, ends, 0.0)
        spread = jnp.broadcast_to(ends[:, None, :], (HEADS_LOCAL, CHANNELS, SPAN))
        spread = spread.reshape(HEADS_LOCAL * CHANNELS, SPAN)
        turned = x[p].astype(f32).T
        state = jnp.dot(
            (turned * spread).astype(bf16), writes[p], preferred_element_type=f32
        )
        passing = jnp.broadcast_to(jnp.exp(last), (HEADS_LOCAL, SPAN))
        passing = jnp.where(last_part == previous, passing, 0.0)
        here = pl.ds(p * rows, rows)
        lower, upper = state[:rows], state[rows:]
        out[here, :] = jnp.where(core == 0, upper, lower).astype(bf16)
        mine[here, :] = jnp.where(core == 0, lower, upper)
        send_decay.append(jnp.where(core == 0, passing[HALF:], passing[:HALF]))
        keep_decay.append(jnp.where(core == 0, passing[:HALF], passing[HALF:]))
    leaving = jnp.concatenate(send_decay, axis=0)
    high = leaving.astype(bf16).astype(f32)
    out[pl.ds(STATE_ROWS, 16), :] = jnp.concatenate([high, leaving - high], axis=0).astype(bf16)
    decay_mine[...] = jnp.concatenate(keep_decay, axis=0)


def unpack(ref):
    tail = ref[pl.ds(STATE_ROWS, 16), :].astype(f32)
    return tail[:8] + tail[8:], ref[pl.ds(0, STATE_ROWS), :].astype(f32)


def scale(decay, state):
    groups = PAIRS * HALF
    return (state.reshape(groups, CHANNELS, STATE) * decay[:, None, :]).reshape(STATE_ROWS, STATE)


def pack(out, decay, state):
    out[pl.ds(0, STATE_ROWS), :] = state.astype(bf16)
    high = decay.astype(bf16).astype(f32)
    out[pl.ds(STATE_ROWS, 16), :] = jnp.concatenate([high, decay - high], axis=0).astype(bf16)


def chip_kernel(meta, got, mine, decay_mine, total, state_first, decay_first):
    core = meta[1]
    decay_got, state_got = unpack(got)
    decay_own, state_own = decay_mine[...], mine[...]
    decay0 = jnp.where(core == 0, decay_own, decay_got)
    decay1 = jnp.where(core == 0, decay_got, decay_own)
    state0 = jnp.where(core == 0, state_own, state_got)
    state1 = jnp.where(core == 0, state_got, state_own)
    state_first[...] = state0
    decay_first[...] = decay0
    pack(total, decay0 * decay1, scale(decay1, state0) + state1)


def line_kernel(meta, own, from1, from2, from3, total, state_before, decay_before):
    zl = meta[4]
    state = jnp.zeros((STATE_ROWS, STATE), f32)
    decay = jnp.ones((PAIRS * HALF, STATE), f32)

    def follow(decay, state, ref, valid):
        factor, fresh = unpack(ref)
        factor = jnp.where(valid, factor, 1.0)
        fresh = jnp.where(valid, fresh, 0.0)
        return decay * factor, scale(factor, state) + fresh

    apart = ((3, from3), (2, from2), (1, from1))
    for d, ref in apart:
        decay, state = follow(decay, state, ref, zl >= d)
    state_before[...] = state
    decay_before[...] = decay
    factor, fresh = unpack(own)
    decay, state = decay * factor, scale(factor, state) + fresh
    for d, ref in apart:
        decay, state = follow(decay, state, ref, zl < d)
    pack(total, decay, state)


def whole_kernel(
    meta, from1, from2, from3, state_before, decay_before, state_first, decay_first, out, keep
):
    core = meta[1]
    state = jnp.zeros((STATE_ROWS, STATE), f32)
    for ref in (from3, from2, from1):
        factor, fresh = unpack(ref)
        state = scale(factor, state) + fresh
    entering = scale(decay_before[...], state) + state_before[...]
    second = scale(decay_first[...], entering) + state_first[...]
    out[...] = jnp.where(core == 0, second, entering).astype(bf16)
    keep[...] = jnp.where(core == 0, entering, second).astype(bf16)


def inside_kernel(
    meta, decay_logs, skip_scale, x, writes, reads, steps, gates, early, late
):
    first = meta[0]
    rates = jnp.exp(head_rows(decay_logs))
    row = lax.broadcasted_iota(jnp.int32, (SPAN, SPAN), 0)
    col = lax.broadcasted_iota(jnp.int32, (SPAN, SPAN), 1)
    upto = jnp.where(row <= col, 1.0, 0.0).astype(f32)
    below = jnp.where(row >= col, 1.0, 0.0).astype(f32)
    for p in range(PAIRS):
        limit = meta[2 + p]
        step = steps[p]
        drop = -rates * step
        cumul = jnp.dot(drop, upto, precision=EXACT, preferred_element_type=f32)
        turned = lax.dot_general(
            below, drop, (((1,), (1,)), ((), ())), precision=EXACT, preferred_element_type=f32
        )
        part_row = jnp.where(first + row >= limit, 1, 0)
        part_col = jnp.where(first + col >= limit, 1, 0)
        previous = jnp.where(first - 1 >= limit, 1, 0)
        allowed = (part_row == part_col) & (row >= col)
        scores = lax.dot_general(
            reads[p], writes[p], (((1,), (1,)), ((), ())), preferred_element_type=f32
        )
        scores = jnp.where(allowed, scores, 0.0)
        reached = jnp.where(part_row[:, :CHANNELS] == previous, 1.0, 0.0)
        for h in range(HEADS_LOCAL):
            here = slice(h * CHANNELS, (h + 1) * CHANNELS)
            column = turned[:, h : h + 1]
            decay = jnp.exp(jnp.minimum(column - cumul[h : h + 1, :], 0.0))
            weights = (scores * decay * step[h : h + 1, :]).astype(bf16)
            inputs = x[p, :, here]
            intra = jnp.dot(weights, inputs, preferred_element_type=f32)
            ssm = intra + skip_scale[h] * inputs.astype(f32)
            gate = gates[p, :, here].astype(f32)
            opened = gate / (1.0 + jnp.exp(-gate))
            early[p, :, here] = ssm * opened
            late[p, :, here] = opened * reached * jnp.exp(column)


def scaled_kernel(weight, gain, out):
    row = lax.broadcasted_iota(jnp.int32, (SPAN, SPAN), 0)
    col = lax.broadcasted_iota(jnp.int32, (SPAN, SPAN), 1)
    for part in range(WIDTH // SPAN):
        here = pl.ds(part * SPAN, SPAN)
        gains = jnp.broadcast_to(gain[:, part * SPAN : (part + 1) * SPAN], (SPAN, SPAN))
        turned = jnp.sum(jnp.where(row == col, gains, 0.0), axis=1, keepdims=True)
        out[here, :] = (weight[here, :].astype(f32) * turned).astype(bf16)


def hidden_kernel(meta, keep, got, reads, early, late, *outs):
    core = meta[1]
    rows = HALF * CHANNELS
    for p, out in enumerate(outs):
        here = pl.ds(p * rows, rows)
        own, other = keep[here, :], got[here, :]
        for half in range(2):
            state = jnp.where(core == half, own, other)
            columns = slice(half * rows, (half + 1) * rows)
            carry = lax.dot_general(
                reads[p], state, (((1,), (1,)), ((), ())), preferred_element_type=f32
            )
            gated = early[p, :, columns] + late[p, :, columns] * carry
            out[:, columns] = gated.astype(bf16)


def arrange_kernel(meta, spot, *refs):
    chunks, hidden, tails = refs[: PAIRS * NZH], refs[-2], refs[-1]
    zh = meta[5]
    ones = jnp.ones((8, WIDTH), f32)
    for p in range(PAIRS):
        here = pl.ds(p * SPAN, SPAN)
        total = jnp.zeros((SPAN, WIDTH), f32)
        for k, move in enumerate((0, NZH - 1, 1, 2)):
            chunk = chunks[PAIRS * k + p][...]
            turn = spot[zh * NZH + (zh + move) % NZH]
            columns = pl.ds(pl.multiple_of(turn * WIDTH, WIDTH), WIDTH)
            hidden[here, columns] = chunk
            wide = chunk.astype(f32)
            total += wide * wide
        squares = lax.dot_general(
            ones, total, (((1,), (1,)), ((), ())), precision=EXACT, preferred_element_type=f32
        )
        high = squares.astype(bf16).astype(f32)
        for place, part in ((p * SPAN, high), (TOKENS + p * SPAN, squares - high)):
            tails[:, pl.ds(place, SPAN)] = jnp.concatenate([part, part], axis=0).astype(bf16)


def project_kernel(index, hidden, tails, weight, out):
    half = WIDTH // 2
    for core in range(NCORE):
        total = jnp.dot(hidden[...], weight[index[0], core], preferred_element_type=f32)
        out[pl.ds(0, TOKENS), pl.ds(core * half, half)] = total.astype(bf16)
    out[pl.ds(TOKENS, 16), :] = tails[...]


def finish_kernel(own, got1, got2, got3, out):
    refs = (own, got1, got2, got3)
    row = lax.broadcasted_iota(jnp.int32, (SPAN, SPAN), 0)
    col = lax.broadcasted_iota(jnp.int32, (SPAN, SPAN), 1)
    tail = pl.ds(TOKENS, 16)
    both = sum(ref[tail, :].astype(f32) for ref in refs)
    squares = both[:1, :TOKENS] + both[:1, TOKENS:]
    factor = lax.rsqrt(squares / INNER + EPSILON)
    for p in range(PAIRS):
        here = pl.ds(p * SPAN, SPAN)
        spread = jnp.broadcast_to(factor[:, p * SPAN : (p + 1) * SPAN], (SPAN, SPAN))
        turned = jnp.sum(jnp.where(row == col, spread, 0.0), axis=1, keepdims=True)
        total = sum(ref[here, :].astype(f32) for ref in refs)
        out[p] = (total * turned).astype(bf16)


def shards(
    head_inputs,
    gate_inputs,
    write_vectors,
    read_vectors,
    step_sizes,
    decay_logs,
    skip_scale,
    norm_gain,
    out_weight,
    boundary,
):
    seq, head = lax.axis_index("seq"), lax.axis_index("head")
    zl, core = (seq // NCORE) % NZL, seq % NCORE
    y, zh = head // NZH, head % NZH
    first = seq * SPAN
    meta = jnp.concatenate(
        [jnp.stack([first, core]).astype(jnp.int32), boundary, jnp.stack([zl, zh, y]).astype(jnp.int32)]
    )

    group = head // 2
    writes = lax.dynamic_index_in_dim(write_vectors, group, 2, keepdims=False)
    reads = lax.dynamic_index_in_dim(read_vectors, group, 2, keepdims=False)

    payload = shape((PAYLOAD_ROWS, STATE), bf16)
    wide = shape((STATE_ROWS, STATE), f32)
    small = shape((PAIRS * HALF, STATE), f32)
    scaled = call(
        scaled_kernel,
        shape((WIDTH, WIDTH // 2), bf16),
        [VMEM, VMEM],
        (out_weight, norm_gain.reshape(1, WIDTH)),
        2**18,
        2**19,
    )
    near = swap_z(scaled)
    leaving, mine, decay_mine = call(
        states_kernel,
        (payload, wide, small),
        [SMEM, SMEM, VMEM, VMEM, VMEM],
        (meta, decay_logs, head_inputs, writes, step_sizes),
        2 * 2**24,
        2**20,
    )
    total, state_first, decay_first = call(
        chip_kernel,
        (payload, wide, small),
        [SMEM, VMEM, VMEM, VMEM],
        (meta, to_core(leaving), mine, decay_mine),
        2**18,
        2**19,
    )
    local = shape((PAIRS, SPAN, WIDTH), f32)
    early, late = call(
        inside_kernel,
        (local, local),
        [SMEM, SMEM, SMEM] + [VMEM] * 5,
        (meta, decay_logs, skip_scale, head_inputs, writes, reads, step_sizes, gate_inputs),
        2**26,
        2**21,
    )
    near, total = lax.optimization_barrier((near, total))
    from_zl = [to_zl(total, d) for d in (1, 2, 3)]
    early, *from_zl = lax.optimization_barrier((early, *from_zl))
    line, state_before, decay_before = call(
        line_kernel,
        (payload, wide, small),
        [SMEM] + [VMEM] * 4,
        (meta, total, *from_zl),
        2**18,
        2**19,
    )
    from_x = [to_x(line, d) for d in (1, 2, 3)]
    half_state = shape((STATE_ROWS, STATE), bf16)
    crossing, keep = call(
        whole_kernel,
        (half_state, half_state),
        [SMEM] + [VMEM] * 7,
        (meta, *from_x)
        + (state_before, decay_before, state_first, decay_first),
        2**18,
        2**19,
    )
    got = to_core(crossing)

    token_part = shape((SPAN, WIDTH), bf16)
    first, second = call(
        hidden_kernel,
        (token_part, token_part),
        [SMEM] + [VMEM] * 5,
        (meta, keep, got, reads, early, late),
        2**25,
        2**21,
    )
    line_weight = gather(near, lambda x, zl, core: (x, core))
    line_weight, first, second = lax.optimization_barrier((line_weight, first, second))
    weight = gather(line_weight, lambda x, zl, core: zl)
    weight = weight.reshape(NX, NCORE, NZH * WIDTH, WIDTH // 2)

    first_below, second_above = to_zh(first, 1), to_zh(second, NZH - 1)
    second_below, first_above = to_zh(second, 1), to_zh(first, NZH - 1)
    far = (to_zh(first_below, 1), to_zh(second_above, NZH - 1))
    chunks = (first, second, first_below, second_below, first_above, second_above) + far
    places = jnp.array(SPOT, jnp.int32).reshape(-1)
    arranged, tails = call(
        arrange_kernel,
        (shape((TOKENS, NZH * WIDTH), bf16), shape((16, WIDTH), bf16)),
        [SMEM, SMEM] + [VMEM] * PAIRS * NZH,
        (meta, places, *chunks),
        2**24,
        2**21,
    )
    def partial(d):
        return call(
            project_kernel,
            shape((TOKEN_ROWS, WIDTH), bf16),
            [SMEM] + [VMEM] * 3,
            (((y + d) % NY).reshape(1), arranged, tails, weight),
            2**29,
            2**21,
            (),
            24 * 2**20,
        )

    arrived = [to_y(partial(d), d) for d in (2, 1, 3)]
    return call(
        finish_kernel,
        shape((PAIRS, SPAN, WIDTH), bf16),
        [VMEM] * 4,
        (partial(0), *arrived),
        2**20,
        2**20,
    )


def solution(mesh):
    return jax.shard_map(
        shards,
        mesh=mesh,
        in_specs=(
            P(None, "seq", "head"),
            P(None, "seq", "head"),
            P(None, "seq", None, None),
            P(None, "seq", None, None),
            P(None, "head", "seq"),
            P("head"),
            P("head"),
            P("head"),
            P("head", "seq"),
            P(),
        ),
        out_specs=P(None, "seq", "head"),
        check_vma=False,
    )
```

```python
import jax
import jax.numpy as jnp
from jax import lax
from jax.experimental import pallas as pl
from jax.experimental.pallas import tpu as pltpu
from jax.sharding import PartitionSpec as P

INNER = 8192
EPSILON = 1e-05
PAIRS = 2
SPAN = 128
HEADS_LOCAL = 8
HALF = 4
CHANNELS = 64
STATE = 128
WIDTH = 512
TOKENS = PAIRS * SPAN
STATE_ROWS = PAIRS * HALF * CHANNELS
PAYLOAD_ROWS = STATE_ROWS + 16
SPOT = ((0, 2, 3, 1), (1, 2, 3, 0), (3, 0, 1, 2), (2, 0, 1, 3))
TOKEN_ROWS = TOKENS + 16
NX = NZL = NY = NZH = 4
NCORE = 2
EXACT = lax.Precision.HIGHEST
f32 = jnp.float32
bf16 = jnp.bfloat16


def seq_index(x, zl, core):
    return (x * NZL + zl) * NCORE + core


def head_index(y, zh):
    return y * NZH + zh


def route(move):
    pairs = []
    for x in range(NX):
        for zl in range(NZL):
            for core in range(NCORE):
                for y in range(NY):
                    for zh in range(NZH):
                        to = move(x, zl, core, y, zh)
                        if to is None:
                            continue
                        source = seq_index(x, zl, core) * NY * NZH + head_index(y, zh)
                        target = seq_index(*to[:3]) * NY * NZH + head_index(*to[3:])
                        pairs.append((source, target))
    return pairs


def send(value, move):
    return lax.ppermute(value, ("seq", "head"), route(move))


def to_core(value):
    return send(value, lambda x, zl, c, y, zh: (x, zl, 1 - c, y, zh))


def to_zl(value, d):
    return send(value, lambda x, zl, c, y, zh: (x, (zl + d) % NZL, c, y, zh))


def to_x(value, d):
    return send(value, lambda x, zl, c, y, zh: (x + d, zl, c, y, zh) if x + d < NX else None)


def to_y(value, d):
    return send(value, lambda x, zl, c, y, zh: (x, zl, c, (y + d) % NY, zh))


def to_zh(value, d):
    return send(value, lambda x, zl, c, y, zh: (x, zl, c, y, (zh + d) % NZH))


def swap_z(value):
    return send(value, lambda x, zl, c, y, zh: (x, SPOT[zl][zh], c, y, zl))


def gather(block, key):
    groups = {}
    for x in range(NX):
        for zl in range(NZL):
            for core in range(NCORE):
                groups.setdefault(key(x, zl, core), []).append(seq_index(x, zl, core))
    return lax.all_gather(
        block, "seq", axis=0, tiled=True, axis_index_groups=list(groups.values())
    )


VMEM = pl.BlockSpec(memory_space=pltpu.VMEM)
SMEM = pl.BlockSpec(memory_space=pltpu.SMEM)


def call(kernel, outs, specs, args, flops, moved, scratch=(), limit=16 * 2**20):
    return pl.pallas_call(
        kernel,
        out_shape=outs,
        in_specs=specs,
        out_specs=jax.tree.map(lambda _: VMEM, outs),
        scratch_shapes=scratch,
        cost_estimate=pl.CostEstimate(flops=flops, bytes_accessed=moved, transcendentals=0),
        compiler_params=pltpu.CompilerParams(vmem_limit_bytes=limit),
    )(*args)


def shape(dims, kind):
    return jax.ShapeDtypeStruct(dims, kind)


def head_rows(scalars):
    rows = lax.broadcasted_iota(jnp.int32, (HEADS_LOCAL, SPAN), 0)
    out = jnp.zeros((HEADS_LOCAL, SPAN), f32)
    for h in range(HEADS_LOCAL):
        out = jnp.where(rows == h, scalars[h], out)
    return out


def states_kernel(meta, decay_logs, x, writes, steps, out, mine, decay_mine):
    first, core = meta[0], meta[1]
    rates = jnp.exp(head_rows(decay_logs))
    row = lax.broadcasted_iota(jnp.int32, (SPAN, SPAN), 0)
    col = lax.broadcasted_iota(jnp.int32, (SPAN, SPAN), 1)
    upto = jnp.where(row <= col, 1.0, 0.0).astype(f32)
    position = first + lax.broadcasted_iota(jnp.int32, (HEADS_LOCAL, SPAN), 1)
    send_decay, keep_decay = [], []
    rows = HALF * CHANNELS
    for p in range(PAIRS):
        limit = meta[2 + p]
        step = steps[p]
        cumul = jnp.dot(-rates * step, upto, precision=EXACT, preferred_element_type=f32)
        last = cumul[:, SPAN - 1 :]
        last_part = jnp.where(first + SPAN - 1 >= limit, 1, 0)
        previous = jnp.where(first - 1 >= limit, 1, 0)
        part = jnp.where(position >= limit, 1, 0)
        ends = jnp.exp(last - cumul) * step
        ends = jnp.where(part == last_part, ends, 0.0)
        spread = jnp.broadcast_to(ends[:, None, :], (HEADS_LOCAL, CHANNELS, SPAN))
        spread = spread.reshape(HEADS_LOCAL * CHANNELS, SPAN)
        turned = x[p].astype(f32).T
        state = jnp.dot(
            (turned * spread).astype(bf16), writes[p], preferred_element_type=f32
        )
        passing = jnp.broadcast_to(jnp.exp(last), (HEADS_LOCAL, SPAN))
        passing = jnp.where(last_part == previous, passing, 0.0)
        here = pl.ds(p * rows, rows)
        lower, upper = state[:rows], state[rows:]
        out[here, :] = jnp.where(core == 0, upper, lower).astype(bf16)
        mine[here, :] = jnp.where(core == 0, lower, upper)
        send_decay.append(jnp.where(core == 0, passing[HALF:], passing[:HALF]))
        keep_decay.append(jnp.where(core == 0, passing[:HALF], passing[HALF:]))
    leaving = jnp.concatenate(send_decay, axis=0)
    high = leaving.astype(bf16).astype(f32)
    out[pl.ds(STATE_ROWS, 16), :] = jnp.concatenate([high, leaving - high], axis=0).astype(bf16)
    decay_mine[...] = jnp.concatenate(keep_decay, axis=0)


def unpack(ref):
    tail = ref[pl.ds(STATE_ROWS, 16), :].astype(f32)
    return tail[:8] + tail[8:], ref[pl.ds(0, STATE_ROWS), :].astype(f32)


def scale(decay, state):
    groups = PAIRS * HALF
    return (state.reshape(groups, CHANNELS, STATE) * decay[:, None, :]).reshape(STATE_ROWS, STATE)


def pack(out, decay, state):
    out[pl.ds(0, STATE_ROWS), :] = state.astype(bf16)
    high = decay.astype(bf16).astype(f32)
    out[pl.ds(STATE_ROWS, 16), :] = jnp.concatenate([high, decay - high], axis=0).astype(bf16)


def chip_kernel(meta, got, mine, decay_mine, total, state_first, decay_first):
    core = meta[1]
    decay_got, state_got = unpack(got)
    decay_own, state_own = decay_mine[...], mine[...]
    decay0 = jnp.where(core == 0, decay_own, decay_got)
    decay1 = jnp.where(core == 0, decay_got, decay_own)
    state0 = jnp.where(core == 0, state_own, state_got)
    state1 = jnp.where(core == 0, state_got, state_own)
    state_first[...] = state0
    decay_first[...] = decay0
    pack(total, decay0 * decay1, scale(decay1, state0) + state1)


def line_kernel(meta, own, from1, from2, from3, total, state_before, decay_before):
    zl = meta[4]
    state = jnp.zeros((STATE_ROWS, STATE), f32)
    decay = jnp.ones((PAIRS * HALF, STATE), f32)

    def follow(decay, state, ref, valid):
        factor, fresh = unpack(ref)
        factor = jnp.where(valid, factor, 1.0)
        fresh = jnp.where(valid, fresh, 0.0)
        return decay * factor, scale(factor, state) + fresh

    apart = ((3, from3), (2, from2), (1, from1))
    for d, ref in apart:
        decay, state = follow(decay, state, ref, zl >= d)
    state_before[...] = state
    decay_before[...] = decay
    factor, fresh = unpack(own)
    decay, state = decay * factor, scale(factor, state) + fresh
    for d, ref in apart:
        decay, state = follow(decay, state, ref, zl < d)
    pack(total, decay, state)


def whole_kernel(
    meta, from1, from2, from3, state_before, decay_before, state_first, decay_first, out, keep
):
    core = meta[1]
    state = jnp.zeros((STATE_ROWS, STATE), f32)
    for ref in (from3, from2, from1):
        factor, fresh = unpack(ref)
        state = scale(factor, state) + fresh
    entering = scale(decay_before[...], state) + state_before[...]
    second = scale(decay_first[...], entering) + state_first[...]
    out[...] = jnp.where(core == 0, second, entering).astype(bf16)
    keep[...] = jnp.where(core == 0, entering, second).astype(bf16)


def inside_kernel(
    meta, decay_logs, skip_scale, x, writes, reads, steps, gates, early, late
):
    first = meta[0]
    rates = jnp.exp(head_rows(decay_logs))
    row = lax.broadcasted_iota(jnp.int32, (SPAN, SPAN), 0)
    col = lax.broadcasted_iota(jnp.int32, (SPAN, SPAN), 1)
    upto = jnp.where(row <= col, 1.0, 0.0).astype(f32)
    below = jnp.where(row >= col, 1.0, 0.0).astype(f32)
    for p in range(PAIRS):
        limit = meta[2 + p]
        step = steps[p]
        drop = -rates * step
        cumul = jnp.dot(drop, upto, precision=EXACT, preferred_element_type=f32)
        turned = lax.dot_general(
            below, drop, (((1,), (1,)), ((), ())), precision=EXACT, preferred_element_type=f32
        )
        part_row = jnp.where(first + row >= limit, 1, 0)
        part_col = jnp.where(first + col >= limit, 1, 0)
        previous = jnp.where(first - 1 >= limit, 1, 0)
        allowed = (part_row == part_col) & (row >= col)
        scores = lax.dot_general(
            reads[p], writes[p], (((1,), (1,)), ((), ())), preferred_element_type=f32
        )
        scores = jnp.where(allowed, scores, 0.0)
        reached = jnp.where(part_row[:, :CHANNELS] == previous, 1.0, 0.0)
        for h in range(HEADS_LOCAL):
            here = slice(h * CHANNELS, (h + 1) * CHANNELS)
            column = turned[:, h : h + 1]
            decay = jnp.exp(jnp.minimum(column - cumul[h : h + 1, :], 0.0))
            weights = (scores * decay * step[h : h + 1, :]).astype(bf16)
            inputs = x[p, :, here]
            intra = jnp.dot(weights, inputs, preferred_element_type=f32)
            ssm = intra + skip_scale[h] * inputs.astype(f32)
            gate = gates[p, :, here].astype(f32)
            opened = gate / (1.0 + jnp.exp(-gate))
            early[p, :, here] = ssm * opened
            late[p, :, here] = opened * reached * jnp.exp(column)


def scaled_kernel(weight, gain, out):
    row = lax.broadcasted_iota(jnp.int32, (SPAN, SPAN), 0)
    col = lax.broadcasted_iota(jnp.int32, (SPAN, SPAN), 1)
    for part in range(WIDTH // SPAN):
        here = pl.ds(part * SPAN, SPAN)
        gains = jnp.broadcast_to(gain[:, part * SPAN : (part + 1) * SPAN], (SPAN, SPAN))
        turned = jnp.sum(jnp.where(row == col, gains, 0.0), axis=1, keepdims=True)
        out[here, :] = (weight[here, :].astype(f32) * turned).astype(bf16)


def hidden_kernel(meta, keep, got, reads, early, late, *outs):
    core = meta[1]
    rows = HALF * CHANNELS
    for p, out in enumerate(outs):
        here = pl.ds(p * rows, rows)
        own, other = keep[here, :], got[here, :]
        for half in range(2):
            state = jnp.where(core == half, own, other)
            columns = slice(half * rows, (half + 1) * rows)
            carry = lax.dot_general(
                reads[p], state, (((1,), (1,)), ((), ())), preferred_element_type=f32
            )
            gated = early[p, :, columns] + late[p, :, columns] * carry
            out[:, columns] = gated.astype(bf16)


def arrange_kernel(meta, spot, *refs):
    chunks, hidden, tails = refs[: PAIRS * NZH], refs[-2], refs[-1]
    zh = meta[5]
    ones = jnp.ones((8, WIDTH), f32)
    for p in range(PAIRS):
        here = pl.ds(p * SPAN, SPAN)
        total = jnp.zeros((SPAN, WIDTH), f32)
        for k, move in enumerate((0, NZH - 1, 1, 2)):
            chunk = chunks[PAIRS * k + p][...]
            turn = spot[zh * NZH + (zh + move) % NZH]
            columns = pl.ds(pl.multiple_of(turn * WIDTH, WIDTH), WIDTH)
            hidden[here, columns] = chunk
            wide = chunk.astype(f32)
            total += wide * wide
        squares = lax.dot_general(
            ones, total, (((1,), (1,)), ((), ())), precision=EXACT, preferred_element_type=f32
        )
        high = squares.astype(bf16).astype(f32)
        for place, part in ((p * SPAN, high), (TOKENS + p * SPAN, squares - high)):
            tails[:, pl.ds(place, SPAN)] = jnp.concatenate([part, part], axis=0).astype(bf16)


def project_kernel(index, hidden, tails, weight, out):
    half = WIDTH // 2
    for core in range(NCORE):
        total = jnp.dot(hidden[...], weight[index[0], core], preferred_element_type=f32)
        out[pl.ds(0, TOKENS), pl.ds(core * half, half)] = total.astype(bf16)
    out[pl.ds(TOKENS, 16), :] = tails[...]


def finish_kernel(own, got1, got2, got3, out):
    refs = (own, got1, got2, got3)
    row = lax.broadcasted_iota(jnp.int32, (SPAN, SPAN), 0)
    col = lax.broadcasted_iota(jnp.int32, (SPAN, SPAN), 1)
    tail = pl.ds(TOKENS, 16)
    both = sum(ref[tail, :].astype(f32) for ref in refs)
    squares = both[:1, :TOKENS] + both[:1, TOKENS:]
    factor = lax.rsqrt(squares / INNER + EPSILON)
    for p in range(PAIRS):
        here = pl.ds(p * SPAN, SPAN)
        spread = jnp.broadcast_to(factor[:, p * SPAN : (p + 1) * SPAN], (SPAN, SPAN))
        turned = jnp.sum(jnp.where(row == col, spread, 0.0), axis=1, keepdims=True)
        total = sum(ref[here, :].astype(f32) for ref in refs)
        out[p] = (total * turned).astype(bf16)


def shards(
    head_inputs,
    gate_inputs,
    write_vectors,
    read_vectors,
    step_sizes,
    decay_logs,
    skip_scale,
    norm_gain,
    out_weight,
    boundary,
):
    seq, head = lax.axis_index("seq"), lax.axis_index("head")
    zl, core = (seq // NCORE) % NZL, seq % NCORE
    y, zh = head // NZH, head % NZH
    first = seq * SPAN
    meta = jnp.concatenate(
        [jnp.stack([first, core]).astype(jnp.int32), boundary, jnp.stack([zl, zh, y]).astype(jnp.int32)]
    )

    group = head // 2
    writes = lax.dynamic_index_in_dim(write_vectors, group, 2, keepdims=False)
    reads = lax.dynamic_index_in_dim(read_vectors, group, 2, keepdims=False)

    payload = shape((PAYLOAD_ROWS, STATE), bf16)
    wide = shape((STATE_ROWS, STATE), f32)
    small = shape((PAIRS * HALF, STATE), f32)
    scaled = call(
        scaled_kernel,
        shape((WIDTH, WIDTH // 2), bf16),
        [VMEM, VMEM],
        (out_weight, norm_gain.reshape(1, WIDTH)),
        2**18,
        2**19,
    )
    near = swap_z(scaled)
    leaving, mine, decay_mine = call(
        states_kernel,
        (payload, wide, small),
        [SMEM, SMEM, VMEM, VMEM, VMEM],
        (meta, decay_logs, head_inputs, writes, step_sizes),
        2 * 2**24,
        2**20,
    )
    total, state_first, decay_first = call(
        chip_kernel,
        (payload, wide, small),
        [SMEM, VMEM, VMEM, VMEM],
        (meta, to_core(leaving), mine, decay_mine),
        2**18,
        2**19,
    )
    local = shape((PAIRS, SPAN, WIDTH), f32)
    early, late = call(
        inside_kernel,
        (local, local),
        [SMEM, SMEM, SMEM] + [VMEM] * 5,
        (meta, decay_logs, skip_scale, head_inputs, writes, reads, step_sizes, gate_inputs),
        2**26,
        2**21,
    )
    near, total = lax.optimization_barrier((near, total))
    from_zl = [to_zl(total, d) for d in (1, 2, 3)]
    early, *from_zl = lax.optimization_barrier((early, *from_zl))
    line, state_before, decay_before = call(
        line_kernel,
        (payload, wide, small),
        [SMEM] + [VMEM] * 4,
        (meta, total, *from_zl),
        2**18,
        2**19,
    )
    from_x = [to_x(line, d) for d in (1, 2, 3)]
    half_state = shape((STATE_ROWS, STATE), bf16)
    crossing, keep = call(
        whole_kernel,
        (half_state, half_state),
        [SMEM] + [VMEM] * 7,
        (meta, *from_x)
        + (state_before, decay_before, state_first, decay_first),
        2**18,
        2**19,
    )
    got = to_core(crossing)

    token_part = shape((SPAN, WIDTH), bf16)
    first, second = call(
        hidden_kernel,
        (token_part, token_part),
        [SMEM] + [VMEM] * 5,
        (meta, keep, got, reads, early, late),
        2**25,
        2**21,
    )
    line_weight = gather(near, lambda x, zl, core: (x, core))
    line_weight, first, second = lax.optimization_barrier((line_weight, first, second))
    weight = gather(line_weight, lambda x, zl, core: zl)
    weight = weight.reshape(NX, NCORE, NZH * WIDTH, WIDTH // 2)

    first_below, second_above = to_zh(first, 1), to_zh(second, NZH - 1)
    second_below, first_above = to_zh(second, 1), to_zh(first, NZH - 1)
    far = (to_zh(first_below, 1), to_zh(second_above, NZH - 1))
    chunks = (first, second, first_below, second_below, first_above, second_above) + far
    places = jnp.array(SPOT, jnp.int32).reshape(-1)
    arranged, tails = call(
        arrange_kernel,
        (shape((TOKENS, NZH * WIDTH), bf16), shape((16, WIDTH), bf16)),
        [SMEM, SMEM] + [VMEM] * PAIRS * NZH,
        (meta, places, *chunks),
        2**24,
        2**21,
    )
    def partial(target, weights, flops=2**29):
        return call(
            project_kernel,
            shape((TOKEN_ROWS, WIDTH), bf16),
            [SMEM] + [VMEM] * 3,
            (target.reshape(1), arranged, tails, weights),
            flops,
            2**21,
            (),
            24 * 2**20,
        )

    first_weight = lax.dynamic_slice_in_dim(weight, (y + 2) % NY, 1, 0)
    sent = to_y(partial(jnp.zeros((), jnp.int32), first_weight, 2**33), 2)
    arrived = [sent] + [to_y(partial((y + d) % NY, weight), d) for d in (1, 3)]
    return call(
        finish_kernel,
        shape((PAIRS, SPAN, WIDTH), bf16),
        [VMEM] * 4,
        (partial(y, weight), *arrived),
        2**20,
        2**20,
    )


def solution(mesh):
    return jax.shard_map(
        shards,
        mesh=mesh,
        in_specs=(
            P(None, "seq", "head"),
            P(None, "seq", "head"),
            P(None, "seq", None, None),
            P(None, "seq", None, None),
            P(None, "head", "seq"),
            P("head"),
            P("head"),
            P("head"),
            P("head", "seq"),
            P(),
        ),
        out_specs=P(None, "seq", "head"),
        check_vma=False,
    )
```

```python
import jax
import jax.numpy as jnp
from jax import lax
from jax.experimental import pallas as pl
from jax.experimental.pallas import tpu as pltpu
from jax.sharding import PartitionSpec as P

INNER = 8192
EPSILON = 1e-05
PAIRS = 2
SPAN = 128
HEADS_LOCAL = 8
HALF = 4
CHANNELS = 64
STATE = 128
WIDTH = 512
TOKENS = PAIRS * SPAN
STATE_ROWS = PAIRS * HALF * CHANNELS
PAYLOAD_ROWS = STATE_ROWS + 16
SPOT = ((0, 2, 3, 1), (1, 2, 3, 0), (3, 0, 1, 2), (2, 0, 1, 3))
TOKEN_ROWS = TOKENS + 16
NX = NZL = NY = NZH = 4
NCORE = 2
EXACT = lax.Precision.HIGHEST
f32 = jnp.float32
bf16 = jnp.bfloat16


def seq_index(x, zl, core):
    return (x * NZL + zl) * NCORE + core


def head_index(y, zh):
    return y * NZH + zh


def route(move):
    pairs = []
    for x in range(NX):
        for zl in range(NZL):
            for core in range(NCORE):
                for y in range(NY):
                    for zh in range(NZH):
                        to = move(x, zl, core, y, zh)
                        if to is None:
                            continue
                        source = seq_index(x, zl, core) * NY * NZH + head_index(y, zh)
                        target = seq_index(*to[:3]) * NY * NZH + head_index(*to[3:])
                        pairs.append((source, target))
    return pairs


def send(value, move):
    return lax.ppermute(value, ("seq", "head"), route(move))


def to_core(value):
    return send(value, lambda x, zl, c, y, zh: (x, zl, 1 - c, y, zh))


def to_zl(value, d):
    return send(value, lambda x, zl, c, y, zh: (x, (zl + d) % NZL, c, y, zh))


def to_x(value, d):
    return send(value, lambda x, zl, c, y, zh: (x + d, zl, c, y, zh) if x + d < NX else None)


def to_y(value, d):
    return send(value, lambda x, zl, c, y, zh: (x, zl, c, (y + d) % NY, zh))


def to_zh(value, d):
    return send(value, lambda x, zl, c, y, zh: (x, zl, c, y, (zh + d) % NZH))


def swap_z(value):
    return send(value, lambda x, zl, c, y, zh: (x, SPOT[zl][zh], c, y, zl))


def gather(block, key):
    groups = {}
    for x in range(NX):
        for zl in range(NZL):
            for core in range(NCORE):
                groups.setdefault(key(x, zl, core), []).append(seq_index(x, zl, core))
    return lax.all_gather(
        block, "seq", axis=0, tiled=True, axis_index_groups=list(groups.values())
    )


VMEM = pl.BlockSpec(memory_space=pltpu.VMEM)
SMEM = pl.BlockSpec(memory_space=pltpu.SMEM)


def call(kernel, outs, specs, args, flops, moved, scratch=(), limit=16 * 2**20):
    return pl.pallas_call(
        kernel,
        out_shape=outs,
        in_specs=specs,
        out_specs=jax.tree.map(lambda _: VMEM, outs),
        scratch_shapes=scratch,
        cost_estimate=pl.CostEstimate(flops=flops, bytes_accessed=moved, transcendentals=0),
        compiler_params=pltpu.CompilerParams(vmem_limit_bytes=limit),
    )(*args)


def shape(dims, kind):
    return jax.ShapeDtypeStruct(dims, kind)


def head_rows(scalars):
    rows = lax.broadcasted_iota(jnp.int32, (HEADS_LOCAL, SPAN), 0)
    out = jnp.zeros((HEADS_LOCAL, SPAN), f32)
    for h in range(HEADS_LOCAL):
        out = jnp.where(rows == h, scalars[h], out)
    return out


def states_kernel(meta, decay_logs, x, writes, steps, out, mine, decay_mine):
    first, core = meta[0], meta[1]
    rates = jnp.exp(head_rows(decay_logs))
    row = lax.broadcasted_iota(jnp.int32, (SPAN, SPAN), 0)
    col = lax.broadcasted_iota(jnp.int32, (SPAN, SPAN), 1)
    upto = jnp.where(row <= col, 1.0, 0.0).astype(f32)
    position = first + lax.broadcasted_iota(jnp.int32, (HEADS_LOCAL, SPAN), 1)
    send_decay, keep_decay = [], []
    rows = HALF * CHANNELS
    for p in range(PAIRS):
        limit = meta[2 + p]
        step = steps[p]
        cumul = jnp.dot(-rates * step, upto, precision=EXACT, preferred_element_type=f32)
        last = cumul[:, SPAN - 1 :]
        last_part = jnp.where(first + SPAN - 1 >= limit, 1, 0)
        previous = jnp.where(first - 1 >= limit, 1, 0)
        part = jnp.where(position >= limit, 1, 0)
        ends = jnp.exp(last - cumul) * step
        ends = jnp.where(part == last_part, ends, 0.0)
        spread = jnp.broadcast_to(ends[:, None, :], (HEADS_LOCAL, CHANNELS, SPAN))
        spread = spread.reshape(HEADS_LOCAL * CHANNELS, SPAN)
        turned = x[p].astype(f32).T
        state = jnp.dot(
            (turned * spread).astype(bf16), writes[p], preferred_element_type=f32
        )
        passing = jnp.broadcast_to(jnp.exp(last), (HEADS_LOCAL, SPAN))
        passing = jnp.where(last_part == previous, passing, 0.0)
        here = pl.ds(p * rows, rows)
        lower, upper = state[:rows], state[rows:]
        out[here, :] = jnp.where(core == 0, upper, lower).astype(bf16)
        mine[here, :] = jnp.where(core == 0, lower, upper)
        send_decay.append(jnp.where(core == 0, passing[HALF:], passing[:HALF]))
        keep_decay.append(jnp.where(core == 0, passing[:HALF], passing[HALF:]))
    leaving = jnp.concatenate(send_decay, axis=0)
    high = leaving.astype(bf16).astype(f32)
    out[pl.ds(STATE_ROWS, 16), :] = jnp.concatenate([high, leaving - high], axis=0).astype(bf16)
    decay_mine[...] = jnp.concatenate(keep_decay, axis=0)


def unpack(ref):
    tail = ref[pl.ds(STATE_ROWS, 16), :].astype(f32)
    return tail[:8] + tail[8:], ref[pl.ds(0, STATE_ROWS), :].astype(f32)


def scale(decay, state):
    groups = PAIRS * HALF
    return (state.reshape(groups, CHANNELS, STATE) * decay[:, None, :]).reshape(STATE_ROWS, STATE)


def pack(out, decay, state):
    out[pl.ds(0, STATE_ROWS), :] = state.astype(bf16)
    high = decay.astype(bf16).astype(f32)
    out[pl.ds(STATE_ROWS, 16), :] = jnp.concatenate([high, decay - high], axis=0).astype(bf16)


def chip_kernel(meta, got, mine, decay_mine, total, state_first, decay_first):
    core = meta[1]
    decay_got, state_got = unpack(got)
    decay_own, state_own = decay_mine[...], mine[...]
    decay0 = jnp.where(core == 0, decay_own, decay_got)
    decay1 = jnp.where(core == 0, decay_got, decay_own)
    state0 = jnp.where(core == 0, state_own, state_got)
    state1 = jnp.where(core == 0, state_got, state_own)
    state_first[...] = state0
    decay_first[...] = decay0
    pack(total, decay0 * decay1, scale(decay1, state0) + state1)


def line_kernel(meta, own, from1, from2, from3, total, state_before, decay_before):
    zl = meta[4]
    state = jnp.zeros((STATE_ROWS, STATE), f32)
    decay = jnp.ones((PAIRS * HALF, STATE), f32)

    def follow(decay, state, ref, valid):
        factor, fresh = unpack(ref)
        factor = jnp.where(valid, factor, 1.0)
        fresh = jnp.where(valid, fresh, 0.0)
        return decay * factor, scale(factor, state) + fresh

    apart = ((3, from3), (2, from2), (1, from1))
    for d, ref in apart:
        decay, state = follow(decay, state, ref, zl >= d)
    state_before[...] = state
    decay_before[...] = decay
    factor, fresh = unpack(own)
    decay, state = decay * factor, scale(factor, state) + fresh
    for d, ref in apart:
        decay, state = follow(decay, state, ref, zl < d)
    pack(total, decay, state)


def whole_kernel(
    meta, from1, from2, from3, state_before, decay_before, state_first, decay_first, out, keep
):
    core = meta[1]
    state = jnp.zeros((STATE_ROWS, STATE), f32)
    for ref in (from3, from2, from1):
        factor, fresh = unpack(ref)
        state = scale(factor, state) + fresh
    entering = scale(decay_before[...], state) + state_before[...]
    second = scale(decay_first[...], entering) + state_first[...]
    out[...] = jnp.where(core == 0, second, entering).astype(bf16)
    keep[...] = jnp.where(core == 0, entering, second).astype(bf16)


def inside_kernel(
    meta, decay_logs, skip_scale, x, writes, reads, steps, gates, early, late
):
    first = meta[0]
    rates = jnp.exp(head_rows(decay_logs))
    row = lax.broadcasted_iota(jnp.int32, (SPAN, SPAN), 0)
    col = lax.broadcasted_iota(jnp.int32, (SPAN, SPAN), 1)
    upto = jnp.where(row <= col, 1.0, 0.0).astype(f32)
    below = jnp.where(row >= col, 1.0, 0.0).astype(f32)
    for p in range(PAIRS):
        limit = meta[2 + p]
        step = steps[p]
        drop = -rates * step
        cumul = jnp.dot(drop, upto, precision=EXACT, preferred_element_type=f32)
        turned = lax.dot_general(
            below, drop, (((1,), (1,)), ((), ())), precision=EXACT, preferred_element_type=f32
        )
        part_row = jnp.where(first + row >= limit, 1, 0)
        part_col = jnp.where(first + col >= limit, 1, 0)
        previous = jnp.where(first - 1 >= limit, 1, 0)
        allowed = (part_row == part_col) & (row >= col)
        scores = lax.dot_general(
            reads[p], writes[p], (((1,), (1,)), ((), ())), preferred_element_type=f32
        )
        scores = jnp.where(allowed, scores, 0.0)
        reached = jnp.where(part_row[:, :CHANNELS] == previous, 1.0, 0.0)
        for h in range(HEADS_LOCAL):
            here = slice(h * CHANNELS, (h + 1) * CHANNELS)
            column = turned[:, h : h + 1]
            decay = jnp.exp(jnp.minimum(column - cumul[h : h + 1, :], 0.0))
            weights = (scores * decay * step[h : h + 1, :]).astype(bf16)
            inputs = x[p, :, here]
            intra = jnp.dot(weights, inputs, preferred_element_type=f32)
            ssm = intra + skip_scale[h] * inputs.astype(f32)
            gate = gates[p, :, here].astype(f32)
            opened = gate / (1.0 + jnp.exp(-gate))
            early[p, :, here] = ssm * opened
            late[p, :, here] = opened * reached * jnp.exp(column)


def scaled_kernel(weight, gain, out):
    row = lax.broadcasted_iota(jnp.int32, (SPAN, SPAN), 0)
    col = lax.broadcasted_iota(jnp.int32, (SPAN, SPAN), 1)
    for part in range(WIDTH // SPAN):
        here = pl.ds(part * SPAN, SPAN)
        gains = jnp.broadcast_to(gain[:, part * SPAN : (part + 1) * SPAN], (SPAN, SPAN))
        turned = jnp.sum(jnp.where(row == col, gains, 0.0), axis=1, keepdims=True)
        out[here, :] = (weight[here, :].astype(f32) * turned).astype(bf16)


def hidden_kernel(meta, keep, got, reads, early, late, *outs):
    core = meta[1]
    rows = HALF * CHANNELS
    for p, out in enumerate(outs):
        here = pl.ds(p * rows, rows)
        own, other = keep[here, :], got[here, :]
        for half in range(2):
            state = jnp.where(core == half, own, other)
            columns = slice(half * rows, (half + 1) * rows)
            carry = lax.dot_general(
                reads[p], state, (((1,), (1,)), ((), ())), preferred_element_type=f32
            )
            gated = early[p, :, columns] + late[p, :, columns] * carry
            out[:, columns] = gated.astype(bf16)


def arrange_kernel(meta, spot, *refs):
    chunks, hidden, tails = refs[: PAIRS * NZH], refs[-2], refs[-1]
    zh = meta[5]
    ones = jnp.ones((8, WIDTH), f32)
    for p in range(PAIRS):
        here = pl.ds(p * SPAN, SPAN)
        total = jnp.zeros((SPAN, WIDTH), f32)
        for k, move in enumerate((0, NZH - 1, 1, 2)):
            chunk = chunks[PAIRS * k + p][...]
            turn = spot[zh * NZH + (zh + move) % NZH]
            columns = pl.ds(pl.multiple_of(turn * WIDTH, WIDTH), WIDTH)
            hidden[here, columns] = chunk
            wide = chunk.astype(f32)
            total += wide * wide
        squares = lax.dot_general(
            ones, total, (((1,), (1,)), ((), ())), precision=EXACT, preferred_element_type=f32
        )
        high = squares.astype(bf16).astype(f32)
        for place, part in ((p * SPAN, high), (TOKENS + p * SPAN, squares - high)):
            tails[:, pl.ds(place, SPAN)] = jnp.concatenate([part, part], axis=0).astype(bf16)


def project_kernel(index, hidden, tails, weight, out):
    half = WIDTH // 2
    for core in range(NCORE):
        total = jnp.dot(hidden[...], weight[index[0], core], preferred_element_type=f32)
        out[pl.ds(0, TOKENS), pl.ds(core * half, half)] = total.astype(bf16)
    out[pl.ds(TOKENS, 16), :] = tails[...]


def finish_kernel(own, got1, got2, got3, out):
    refs = (own, got1, got2, got3)
    row = lax.broadcasted_iota(jnp.int32, (SPAN, SPAN), 0)
    col = lax.broadcasted_iota(jnp.int32, (SPAN, SPAN), 1)
    tail = pl.ds(TOKENS, 16)
    both = sum(ref[tail, :].astype(f32) for ref in refs)
    squares = both[:1, :TOKENS] + both[:1, TOKENS:]
    factor = lax.rsqrt(squares / INNER + EPSILON)
    for p in range(PAIRS):
        here = pl.ds(p * SPAN, SPAN)
        spread = jnp.broadcast_to(factor[:, p * SPAN : (p + 1) * SPAN], (SPAN, SPAN))
        turned = jnp.sum(jnp.where(row == col, spread, 0.0), axis=1, keepdims=True)
        total = sum(ref[here, :].astype(f32) for ref in refs)
        out[p] = (total * turned).astype(bf16)


def shards(
    head_inputs,
    gate_inputs,
    write_vectors,
    read_vectors,
    step_sizes,
    decay_logs,
    skip_scale,
    norm_gain,
    out_weight,
    boundary,
):
    seq, head = lax.axis_index("seq"), lax.axis_index("head")
    zl, core = (seq // NCORE) % NZL, seq % NCORE
    y, zh = head // NZH, head % NZH
    first = seq * SPAN
    meta = jnp.concatenate(
        [jnp.stack([first, core]).astype(jnp.int32), boundary, jnp.stack([zl, zh, y]).astype(jnp.int32)]
    )

    group = head // 2
    writes = lax.dynamic_index_in_dim(write_vectors, group, 2, keepdims=False)
    reads = lax.dynamic_index_in_dim(read_vectors, group, 2, keepdims=False)

    payload = shape((PAYLOAD_ROWS, STATE), bf16)
    wide = shape((STATE_ROWS, STATE), f32)
    small = shape((PAIRS * HALF, STATE), f32)
    scaled = call(
        scaled_kernel,
        shape((WIDTH, WIDTH // 2), bf16),
        [VMEM, VMEM],
        (out_weight, norm_gain.reshape(1, WIDTH)),
        2**18,
        2**19,
    )
    near = swap_z(scaled)
    leaving, mine, decay_mine = call(
        states_kernel,
        (payload, wide, small),
        [SMEM, SMEM, VMEM, VMEM, VMEM],
        (meta, decay_logs, head_inputs, writes, step_sizes),
        2 * 2**24,
        2**20,
    )
    total, state_first, decay_first = call(
        chip_kernel,
        (payload, wide, small),
        [SMEM, VMEM, VMEM, VMEM],
        (meta, to_core(leaving), mine, decay_mine),
        2**18,
        2**19,
    )
    local = shape((PAIRS, SPAN, WIDTH), f32)
    early, late = call(
        inside_kernel,
        (local, local),
        [SMEM, SMEM, SMEM] + [VMEM] * 5,
        (meta, decay_logs, skip_scale, head_inputs, writes, reads, step_sizes, gate_inputs),
        2**26,
        2**21,
    )
    near, total = lax.optimization_barrier((near, total))
    from_zl = [to_zl(total, d) for d in (1, 2, 3)]
    early, *from_zl = lax.optimization_barrier((early, *from_zl))
    line, state_before, decay_before = call(
        line_kernel,
        (payload, wide, small),
        [SMEM] + [VMEM] * 4,
        (meta, total, *from_zl),
        2**18,
        2**19,
    )
    from_x = [to_x(line, d) for d in (1, 2, 3)]
    half_state = shape((STATE_ROWS, STATE), bf16)
    crossing, keep = call(
        whole_kernel,
        (half_state, half_state),
        [SMEM] + [VMEM] * 7,
        (meta, *from_x)
        + (state_before, decay_before, state_first, decay_first),
        2**18,
        2**19,
    )
    line_weight = gather(near, lambda x, zl, core: (x, core))
    line_weight, crossing = lax.optimization_barrier((line_weight, crossing))
    weight = gather(line_weight, lambda x, zl, core: zl)
    weight = weight.reshape(NX, NCORE, NZH * WIDTH, WIDTH // 2)
    got = to_core(crossing)

    token_part = shape((SPAN, WIDTH), bf16)
    first, second = call(
        hidden_kernel,
        (token_part, token_part),
        [SMEM] + [VMEM] * 5,
        (meta, keep, got, reads, early, late),
        2**25,
        2**21,
    )
    first_below, second_above = to_zh(first, 1), to_zh(second, NZH - 1)
    second_below, first_above = to_zh(second, 1), to_zh(first, NZH - 1)
    far = (to_zh(first_below, 1), to_zh(second_above, NZH - 1))
    chunks = (first, second, first_below, second_below, first_above, second_above) + far
    places = jnp.array(SPOT, jnp.int32).reshape(-1)
    arranged, tails = call(
        arrange_kernel,
        (shape((TOKENS, NZH * WIDTH), bf16), shape((16, WIDTH), bf16)),
        [SMEM, SMEM] + [VMEM] * PAIRS * NZH,
        (meta, places, *chunks),
        2**24,
        2**21,
    )
    def partial(target, weights, flops=2**29):
        return call(
            project_kernel,
            shape((TOKEN_ROWS, WIDTH), bf16),
            [SMEM] + [VMEM] * 3,
            (target.reshape(1), arranged, tails, weights),
            flops,
            2**21,
            (),
            24 * 2**20,
        )

    first_weight = lax.dynamic_slice_in_dim(weight, (y + 2) % NY, 1, 0)
    sent = to_y(partial(jnp.zeros((), jnp.int32), first_weight, 2**33), 2)
    arrived = [sent] + [to_y(partial((y + d) % NY, weight), d) for d in (1, 3)]
    return call(
        finish_kernel,
        shape((PAIRS, SPAN, WIDTH), bf16),
        [VMEM] * 4,
        (partial(y, weight), *arrived),
        2**20,
        2**20,
    )


def solution(mesh):
    return jax.shard_map(
        shards,
        mesh=mesh,
        in_specs=(
            P(None, "seq", "head"),
            P(None, "seq", "head"),
            P(None, "seq", None, None),
            P(None, "seq", None, None),
            P(None, "head", "seq"),
            P("head"),
            P("head"),
            P("head"),
            P("head", "seq"),
            P(),
        ),
        out_specs=P(None, "seq", "head"),
        check_vma=False,
    )
```
